128 devices in a mesh: sec: 2 (over x_hi), row: 16 (over y, x_lo, core), col: 4 (over z).
Axes of the slice: x: 4 (x_hi: 2, x_lo: 2; x = x_hi * 2 + x_lo), y: 4, z: 4, core: 2. Of those that a mesh axis runs over, the one named last changes fastest.
Arguments:
- coarse_state: bfloat16 [720, 78, 1440], P('row', None, ('sec', 'col'))
- row_offset: int32 [1], replicated, may hold values from 1 to 703
- col_offset: int32 [1], replicated, may hold values from 1 to 1375
- fine_static: bfloat16 [256, 4, 1024], P('row', None, ('sec', 'col'))
- w_lift: bfloat16 [78, 256], replicated, may hold values from -0.625 to 0.625
- w_static: bfloat16 [4, 256], replicated, may hold values from -3 to 3
- norm_gains: float32 [4, 256], replicated, may hold values from 0.1 to 1.9
- kernels: bfloat16 [4, 3, 3, 256, 256], replicated, may hold values from -0.125 to 0.125
- w_head: bfloat16 [256, 78], replicated, may hold values from -0.375 to 0.375
- cotangent: bfloat16 [256, 78, 1024], P('row', None, ('sec', 'col')), may hold values from -6 to 6
Outputs:
- fine_out: bfloat16 [256, 78, 1024], P('row', None, ('sec', 'col'))
- coarse_grad: float32 [720, 78, 1440], P('row', None, ('sec', 'col'))
The draws below stay inside these ranges and needn't reach their ends.
Inputs may be any that keep to these rules, and one draw needn't show every extreme that they name: The slab's coarse rows, one before row_offset to 16 after it, lie inside the grid. The slab's coarse columns, one before col_offset to 64 after it, lie inside the grid.
All inputs are finite; a program needn't handle non-finite values.
Results may differ from the reference program's by a relative error of at most 0.015.
Values may be sent and summed in bfloat16 or wider, within the bound.
No kernel may reach another device: no remote copies, remote signals or barrier semaphores. Data moves between devices by JAX's collectives and lax.ppermute only.
A program may use at most 128 MiB of HBM per device.

```python
import jax
import jax.numpy as jnp
from jax import lax

CIN = 78
W = 256
STAT = 4
BLOCKS = 4
R = 16
LAT = 720
LON = 1440
FY = 256
FX = 1024
FPR = 18
FPC = 66


def draw_coarse_state(key, part):
    key = jax.random.fold_in(key, 11)
    key_base, key_chan, key_cell = jax.random.split(key, 3)
    base_draw = jax.random.normal(key_base, (LAT, CIN, LON), jnp.float32)
    channel_scale = jnp.exp(jax.random.uniform(key_chan, (1, CIN, 1), jnp.float32, -1.2, 1.2))
    cell_scale = jax.random.uniform(key_cell, (LAT, 1, LON), jnp.float32, 0.5, 1.5)
    return (base_draw * channel_scale * cell_scale).astype(jnp.bfloat16)


def draw_fine_static(key, part):
    key = jax.random.fold_in(key, 12)
    key_base, key_cell = jax.random.split(key, 2)
    base_draw = jax.random.normal(key_base, (FY, STAT, FX), jnp.float32)
    cell_scale = jnp.exp(jax.random.uniform(key_cell, (FY, 1, FX), jnp.float32, -1.2, 1.2))
    return (base_draw * cell_scale).astype(jnp.bfloat16)


def level_of(own_key, extent, pieces, smallest, high):
    gain, own = 1.0, jax.random.fold_in(own_key, 6)
    for position, blocks in pieces:
        steps = jnp.exp(jax.random.uniform(jax.random.fold_in(own, position), (blocks,), jnp.float32, smallest / len(pieces), high / len(pieces)))
        gain = gain * jnp.repeat(steps, extent[position] // blocks).reshape([-1 if axis == position else 1 for axis in range(len(extent))])
    return gain


def normal_values(rng, dims, width, limit, cuts=(), held_as=jnp.bfloat16):
    array = jax.random.normal(rng, dims, jnp.float32) * width
    if len(cuts) > 0:
        array = level_of(rng, dims, cuts, -0.22, 0.18) * array
    return jnp.clip(array, min=-limit, max=limit).astype(held_as)


def setup_inputs(seed: int = 0) -> dict:
    key_list = jax.random.split(jax.random.key(seed), 11)
    return {
        "coarse_state": draw_coarse_state(jax.random.fold_in(key_list[10], 71), 0),
        "row_offset": jax.random.randint(key_list[1], (1,), 1, LAT - FY // R).astype(jnp.int32),
        "col_offset": jax.random.randint(key_list[2], (1,), 1, LON - FX // R).astype(jnp.int32),
        "fine_static": draw_fine_static(jax.random.fold_in(key_list[10], 71), 0),
        "w_lift": normal_values(key_list[4], (CIN, W), CIN ** -0.5, 0.625),
        "w_static": normal_values(key_list[5], (STAT, W), STAT ** -0.5, 3.0),
        "norm_gains": jnp.clip(1.0 + 0.18 * jax.random.normal(key_list[6], (BLOCKS, W), jnp.float32), 0.1, 1.9),
        "kernels": normal_values(key_list[7], (BLOCKS, 3, 3, W, W), (9 * W) ** -0.5, 0.125),
        "w_head": normal_values(key_list[8], (W, CIN), W ** -0.5, 0.375),
        "cotangent": normal_values(key_list[9], (FY, CIN, FX), 1.0, 6.0, ((0, 16), (2, 8))),
    }


def interp_matrix(fine_len, ratio_cells):
    fine_idx = jnp.arange(fine_len, dtype=jnp.int32)
    numerator = 2 * fine_idx + 1 + ratio_cells
    lower_row = numerator // (2 * ratio_cells)
    weight_hi = (numerator % (2 * ratio_cells)).astype(jnp.float32) / (2.0 * ratio_cells)
    columns = jnp.arange(fine_len // ratio_cells + 2, dtype=jnp.int32)
    below_hot = (columns[None, :] == lower_row[:, None]).astype(jnp.float32)
    above_hot = (columns[None, :] == lower_row[:, None] + 1).astype(jnp.float32)
    return below_hot * (1.0 - weight_hi[:, None]) + above_hot * weight_hi[:, None]

def conv_sum(padded, kernel_set, row_count, col_count, transpose):
    width_out = kernel_set.shape[-1]
    accumulated = jnp.zeros((row_count * col_count, width_out), jnp.float32)
    for offset_dy in range(3):
        for offset_dx in range(3):
            if transpose:
                window = padded[2 - offset_dy:2 - offset_dy + row_count, 2 - offset_dx:2 - offset_dx + col_count, :]
                weight = kernel_set[offset_dy, offset_dx].T
            else:
                window = padded[offset_dy:offset_dy + row_count, offset_dx:offset_dx + col_count, :]
                weight = kernel_set[offset_dy, offset_dx]
            accumulated = accumulated + jnp.dot(window.reshape(row_count * col_count, -1), weight, preferred_element_type=jnp.float32)
    return accumulated.reshape(row_count, col_count, -1)

def normalize(hidden, gain_row):
    hidden_f = hidden.astype(jnp.float32)
    inv_scale = lax.rsqrt(lax.optimization_barrier(jnp.mean(hidden_f * hidden_f, axis=-1, keepdims=True)) + 1e-06)
    return (hidden_f * inv_scale * gain_row[None, None, :], inv_scale)

def norm_backward(hidden, inv_scale, normed, gain_row, conv_back):
    hidden_f = hidden.astype(jnp.float32)
    sigmoid_val = jax.nn.sigmoid(normed)
    scaled_grad = conv_back * sigmoid_val * (1.0 + normed * (1.0 - sigmoid_val)) * gain_row[None, None, :]
    cubed = inv_scale * inv_scale * inv_scale
    return inv_scale * scaled_grad - hidden_f * cubed * lax.optimization_barrier(jnp.mean(hidden_f * scaled_grad, axis=-1, keepdims=True))

def reference(coarse_state, row_offset, col_offset, fine_static, w_lift, w_static, norm_gains, kernels, w_head, cotangent):
    high = lax.Precision.HIGHEST
    first_row = row_offset[0] - 1
    first_col = col_offset[0] - 1
    footprint = lax.dynamic_slice(coarse_state, (first_row, jnp.int32(0), first_col), (FPR, CIN, FPC))
    rows_mat = interp_matrix(FY, R)
    cols_mat = interp_matrix(FX, R)
    partial_up = jnp.einsum('yi,icj->ycj', rows_mat, footprint.astype(jnp.float32), precision=high)
    upsampled = jnp.einsum('ycj,xj->ycx', partial_up, cols_mat, precision=high).astype(jnp.bfloat16)
    hidden = (jnp.einsum('ycx,cw->yxw', upsampled.astype(jnp.float32), w_lift.astype(jnp.float32)) + jnp.einsum('ykx,kw->yxw', fine_static.astype(jnp.float32), w_static.astype(jnp.float32))).astype(jnp.bfloat16)
    saved_hidden = []
    for block_idx in range(BLOCKS):
        saved_hidden.append(hidden)
        normed, inv_scale = normalize(hidden, norm_gains[block_idx])
        activated = (normed * jax.nn.sigmoid(normed)).astype(jnp.bfloat16)
        padded = jnp.pad(activated, ((1, 1), (1, 1), (0, 0)))
        hidden = (hidden.astype(jnp.float32) + conv_sum(padded, kernels[block_idx], FY, FX, False)).astype(jnp.bfloat16)
    fine_out = jnp.einsum('yxw,wc->ycx', hidden.astype(jnp.float32), w_head.astype(jnp.float32)).astype(jnp.bfloat16)
    grad_back = jnp.einsum('ycx,wc->yxw', cotangent.astype(jnp.float32), w_head.astype(jnp.float32))
    for block_idx in reversed(range(BLOCKS)):
        sent = grad_back.astype(jnp.bfloat16)
        padded = jnp.pad(sent, ((1, 1), (1, 1), (0, 0)))
        conv_back = conv_sum(padded, kernels[block_idx], FY, FX, True)
        normed, inv_scale = normalize(saved_hidden[block_idx], norm_gains[block_idx])
        grad_back = grad_back + norm_backward(saved_hidden[block_idx], inv_scale, normed, norm_gains[block_idx], conv_back)
    lifted_back = grad_back.astype(jnp.bfloat16)
    up_back = jnp.einsum('yxw,cw->ycx', lifted_back.astype(jnp.float32), w_lift.astype(jnp.float32))
    window_back = jnp.einsum('yi,ycx->icx', rows_mat, up_back, precision=high)
    window_back = jnp.einsum('icx,xj->icj', window_back, cols_mat, precision=high)
    coarse_grad = lax.dynamic_update_slice(jnp.zeros((LAT, CIN, LON), jnp.float32), window_back, (first_row, jnp.int32(0), first_col))
    return (fine_out, coarse_grad)
```

```python
import functools

import jax
import jax.numpy as jnp
from jax import lax
from jax.experimental import pallas as pl
from jax.experimental.pallas import tpu as pltpu
from jax.sharding import PartitionSpec as P

R = 16
CIN = 78
W = 256
BLOCKS = 4
TR = 16
TC = 128
LAT_DEV = 45
LON_DEV = 180
HR = 6
HC = 8
ER = TR + 2 * HR
L = 9
S = 16
EC = L * S
BF = jnp.bfloat16
F32 = jnp.float32
VM = pl.BlockSpec(memory_space=pltpu.VMEM)
SM = pl.BlockSpec(memory_space=pltpu.SMEM)
MB = 2**20
NT = (((1,), (1,)), ((), ()))
NN = (((1,), (0,)), ((), ()))
TN = (((0,), (0,)), ((), ()))


def dotf(a, b, dims=NN):
    return lax.dot_general(a, b, dims, preferred_element_type=F32)


def iota(shape, dim):
    return lax.broadcasted_iota(jnp.int32, shape, dim)


def ext_col(m):
    return (m & 15) * L + (m >> 4)


def one_hot(cond):
    return jnp.where(cond, 1.0, 0.0).astype(BF)


def col_weight(e, j):
    n = 2 * e + 1
    a = n >> 5
    t = (n & 31).astype(F32) * (1.0 / 32.0)
    return jnp.where(j == a, 1.0 - t, 0.0) + jnp.where(j == a + 1, t, 0.0)


def col_place():
    return lax.axis_index("sec") * 4 + lax.axis_index("col")


def pack_kernel(ro, co, coarse, static, cot, send, xown, pa, pb, prod):
    ri = lax.axis_index("row")
    ci = col_place()
    first_row = ro[0] - 1 - LAT_DEV * ri
    off = co[0] - 1 - LON_DEV * ci
    lj = iota((272, LON_DEV), 1)
    q = iota((272, LON_DEV), 0)
    tail = q - 80
    k = tail >> 6
    c = (tail & 63) >> 3
    s = (tail & 7) - 2 * k
    j_tail = jnp.where((s >= 0) & (s < 2), 8 * c + 8 + s, -100000)
    j = jnp.where(q < 80, jnp.where(q < 66, q, -100000), j_tail)
    sel = one_hot(lj == off + j)

    def row(i, _):
        li = first_row + i
        ok = ((li >= 0) & (li < LAT_DEV)).astype(F32)
        x = coarse[jnp.clip(li, 0, LAT_DEV - 1)]
        prod[i, :, :CIN] = dotf(sel, x, NT) * ok
        return 0

    lax.fori_loop(0, 18, row, 0)

    def dest(r, _):
        tails = prod[r, 80:144] + prod[r + 1, 144:208] + prod[r + 2, 208:272]
        for cc in range(8):
            d = (cc // 4) * 64 + r * 4 + cc % 4
            sl = slice(8 * cc, 8 * cc + 8)
            msg = jnp.concatenate([prod[r, sl], prod[r + 1, sl], prod[r + 2, sl], tails[sl]], axis=0)
            send[d] = msg.astype(BF)
        return 0

    lax.fori_loop(0, 16, dest, 0)
    xown[...] = jnp.zeros_like(xown)
    xown[:, :CIN, :] = cot[...]
    xown[:, 80:84, :] = static[...]
    odd = ri & 1
    pa[...] = xown[pl.ds(jnp.where(odd == 1, 0, TR - HR), HR)]
    pb[...] = xown[pl.ds(jnp.where(odd == 1, TR - HR, 0), HR)]


def pack(ro, co, coarse, static, cot):
    return pl.pallas_call(
        pack_kernel,
        out_shape=[
            jax.ShapeDtypeStruct((128, 32, 128), BF),
            jax.ShapeDtypeStruct((TR, 128, 128), BF),
            jax.ShapeDtypeStruct((HR, 128, 128), BF),
            jax.ShapeDtypeStruct((HR, 128, 128), BF),
        ],
        in_specs=[SM, SM, VM, VM, VM],
        out_specs=[VM] * 4,
        scratch_shapes=[pltpu.VMEM((18, 272, 128), F32)],
        compiler_params=pltpu.CompilerParams(vmem_limit_bytes=32 * MB),
        name="pack",
    )(ro, co, coarse, static, cot)


def edge_kernel(xown, ra, rb, ct, pc, pd, edge):
    ri = lax.axis_index("row")
    ci = col_place()
    m = iota((EC, 128), 0)
    perm = one_hot(ext_col(m) - HC == iota((EC, 128), 1))
    q = iota((16, 128), 0)
    sel = one_hot(iota((16, 128), 1) == jnp.where(q < 8, q, q + 112))
    both = jnp.concatenate([perm, sel], axis=0)

    def do(y, x):
        r = dotf(both, x, NT)
        ct[y] = r[:EC].astype(BF)
        edge[y] = r[EC:]

    def mid(y, _):
        do(y + HR, xown[y])
        return 0

    lax.fori_loop(0, TR, mid, 0)
    odd = (ri & 1) == 1

    def ends(y, _):
        a = ra[y]
        b = rb[y]
        do(y, jnp.where(odd, a, b))
        do(y + HR + TR, jnp.where(odd, b, a))
        return 0

    lax.fori_loop(0, HR, ends, 0)
    oddc = (ci & 1) == 1
    left = edge[:, :8, :].reshape(ER * 8, 128)
    right = edge[:, 8:, :].reshape(ER * 8, 128)
    pc[...] = jnp.where(oddc, left, right).astype(BF)
    pd[...] = jnp.where(oddc, right, left).astype(BF)


def edges(xown, ra, rb):
    return pl.pallas_call(
        edge_kernel,
        out_shape=[
            jax.ShapeDtypeStruct((ER, EC, 128), BF),
            jax.ShapeDtypeStruct((ER * 8, 128), BF),
            jax.ShapeDtypeStruct((ER * 8, 128), BF),
        ],
        in_specs=[VM] * 3,
        out_specs=[VM] * 3,
        scratch_shapes=[pltpu.VMEM((ER, 16, 128), F32)],
        compiler_params=pltpu.CompilerParams(vmem_limit_bytes=16 * MB),
        name="edges",
    )(xown, ra, rb)


def main_kernel(
    recv, ct, rc, rd, wbig, gains, kern, wht, wl, fine, msg,
    vup, hid, act, cv, hs_s, ds_s, back, gsum,
):
    ri = lax.axis_index("row")
    ci = col_place()
    oddc = (ci & 1) == 1

    win = jnp.sum(recv[...].astype(F32), axis=0)
    win = jnp.where(iota((32, 128), 1) < CIN, win, 0.0).astype(BF)
    m = iota((EC, 32), 0)
    q = iota((EC, 32), 1)
    for k in range(3):
        tail = q - 24 - 2 * k
        j = jnp.where((q >= 8 * k) & (q < 8 * k + 8), q - 8 * k, -10)
        j = jnp.where((tail >= 0) & (tail < 2), tail + 8, j)
        coef = col_weight(ext_col(m), j).astype(BF)
        vup[k] = dotf(coef, win)

    m4 = iota((4 * EC, 32), 0)
    q4 = iota((4 * EC, 32), 1)
    y4 = (
        (m4 >= EC).astype(jnp.int32) + (m4 >= 2 * EC).astype(jnp.int32) + (m4 >= 3 * EC).astype(jnp.int32)
    )
    e4 = ext_col(m4 - y4 * EC)
    same = y4 == (q4 >> 3)
    perm_l = one_hot(same & (e4 == (q4 & 7)))
    perm_r = one_hot(same & (e4 - (HC + TC) == (q4 & 7)))

    def lift(g, _):
        rows = pl.ds(pl.multiple_of(g * 32, 32), 32)
        c = rc[rows, :]
        d = rd[rows, :]
        halo = dotf(perm_l, jnp.where(oddc, c, d)) + dotf(perm_r, jnp.where(oddc, d, c))
        ups = []
        for k in range(4):
            n = 2 * (g * 4 + k) + 5
            a = n >> 5
            t = (n & 31).astype(F32) * (1.0 / 32.0)
            ups.append(((1.0 - t) * vup[a] + t * vup[a + 1]).astype(BF))
        up = jnp.concatenate(ups, axis=0)
        own = ct[pl.ds(g * 4, 4)].reshape(4 * EC, 128)
        both = (own.astype(F32) + halo).astype(BF)
        r = dotf(jnp.concatenate([up, both], axis=1), wbig[...])
        hid[pl.ds(g * 4, 4)] = r[:, :W].astype(BF).reshape(4, EC, W)
        back[pl.ds(g * 4, 4)] = r[:, W:].reshape(4, EC, W)
        return 0

    lax.fori_loop(0, ER // 4, lift, 0)

    CK = 48
    col_ok = []
    for ck in range(3):
        gc = ci * TC + ext_col(iota((CK, 1), 0) + ck * CK) - HC
        col_ok.append(jnp.where((gc >= 0) & (gc < 8 * TC), 1.0, 0.0))

    def put(y, ck, v):
        act[y, 1 + 3 * ck : 4 + 3 * ck] = v.astype(BF).reshape(3, S, W)
        if ck == 2:
            act[y, 0] = pltpu.roll(v[32:48], 1, 0).astype(BF)
        if ck == 0:
            act[y, L + 1] = pltpu.roll(v[:16], S - 1, 0).astype(BF)

    def activate(b, y):
        gr = ri * TR + y - HR
        ok = ((gr >= 0) & (gr < 16 * TR)).astype(F32)
        gain = gains[b : b + 1, :]
        for ck in range(3):
            h = hid[y, ck * CK : (ck + 1) * CK, :].astype(F32)
            s = lax.rsqrt(jnp.mean(h * h, axis=-1, keepdims=True) + 1e-06) * (col_ok[ck] * ok)
            hs = h * s
            n = hs * gain
            g = 0.5 * jnp.tanh(0.5 * n) + 0.5
            a = n * g
            put(y, ck, a)
            hs_s[b, y, ck * CK : (ck + 1) * CK, :] = hs.astype(BF)
            ds_s[b, y, ck * CK : (ck + 1) * CK, :] = ((g + a - a * g) * gain * s).astype(BF)

    def conv(b, y0, n, transpose):
        acc = None
        for p in range(3):
            for q in range(3):
                dy = 1 - p if transpose else p - 1
                dx = 2 - q if transpose else q
                x = act[pl.ds(y0 + dy, n), dx : dx + L].reshape(n * EC, W)
                r = dotf(x, kern[b, p, q], NT if transpose else NN)
                acc = r if acc is None else acc + r
        cv[:n] = acc.reshape(n, EC, W)

    def first(y, _):
        activate(0, y)
        return 0

    lax.fori_loop(0, ER, first, 0)

    for b in range(BLOCKS):
        lo, hi = (b + 1, ER - 1 - b) if b < 3 else (HR, HR + TR)
        n = (hi - lo) // 2
        for half in range(2):
            y0 = lo + half * n
            conv(b, y0, n, False)

            def resid(k, _, y0=y0):
                hid[y0 + k] = (hid[y0 + k].astype(F32) + cv[k]).astype(BF)
                return 0

            lax.fori_loop(0, n, resid, 0)
        if b < 3:

            def nxt(y, _, b=b):
                activate(b + 1, y)
                return 0

            lax.fori_loop(lo, hi, nxt, 0)

    perm = one_hot(ext_col(iota((EC, 128), 0)) - HC == iota((EC, 128), 1))

    def head(y, _):
        o = dotf(wht[...], hid[y + HR], NT).astype(BF)
        fine[y] = dotf(o, perm).astype(BF)[:CIN]
        return 0

    lax.fori_loop(0, TR, head, 0)

    def send4(y, _):
        for ck in range(3):
            put(y, ck, back[y, ck * CK : (ck + 1) * CK, :])
        return 0

    lax.fori_loop(2, ER - 2, send4, 0)
    for b in reversed(range(BLOCKS)):
        lo, hi = HR - b, HR + TR + b
        n = (hi - lo) // 2
        for half in range(2):
            y0 = lo + half * n
            conv(b, y0, n, True)

            def grad(k, _, y0=y0, b=b):
                y = y0 + k
                for ck in range(3):
                    sl = slice(ck * CK, (ck + 1) * CK)
                    u = cv[k, sl] * ds_s[b, y, sl].astype(F32)
                    hs = hs_s[b, y, sl].astype(F32)
                    mean = jnp.mean(u * hs, axis=-1, keepdims=True)
                    back[y, sl] = back[y, sl] + (u - hs * mean)
                return 0

            lax.fori_loop(0, n, grad, 0)
        if b > 0:
            lax.fori_loop(lo, hi, send4, 0)

    e = ext_col(iota((32, EC), 1))
    qq = iota((32, EC), 0)
    j = jnp.where(qq < 10, qq, jnp.where(qq < 20, qq - 10, -10))
    own = (e >= HC) & (e < HC + TC)
    cols_t = jnp.where(own, col_weight(e, j), 0.0).astype(BF)
    gsum[...] = jnp.zeros_like(gsum)

    def gather(y, _):
        t = dotf(cols_t, back[y + HR].astype(BF))
        n = 2 * (y + HR) + 5
        a = n >> 5
        w = (n & 31).astype(F32) * (1.0 / 32.0)
        gsum[a] = gsum[a] + (1.0 - w) * t
        gsum[a + 1] = gsum[a + 1] + w * t
        return 0

    lax.fori_loop(0, TR, gather, 0)
    g = jnp.concatenate([gsum[0], gsum[1], gsum[2]], axis=1)
    g_hi = g.astype(BF)
    g_lo = (g - g_hi.astype(F32)).astype(BF)
    o = dotf(g_hi, wl[...]) + dotf(g_lo, wl[...])
    o = jnp.where(iota((32, 128), 0) < 10, o[:, :128], o[:, 128:]).astype(BF)[:24]

    def spread(d, _):
        msg[d] = o
        return 0

    lax.fori_loop(0, 128, spread, 0)


def main(recv, ct, rc, rd, wbig, gains, kern, wht, wl):
    return pl.pallas_call(
        main_kernel,
        out_shape=[
            jax.ShapeDtypeStruct((TR, CIN, TC), BF),
            jax.ShapeDtypeStruct((128, 24, 128), BF),
        ],
        in_specs=[VM] * 9,
        out_specs=[VM] * 2,
        scratch_shapes=[
            pltpu.VMEM((3, EC, 128), F32),
            pltpu.VMEM((ER, EC, W), BF),
            pltpu.VMEM((ER, L + 2, S, W), BF),
            pltpu.VMEM((13, EC, W), F32),
            pltpu.VMEM((BLOCKS, ER, EC, W), BF),
            pltpu.VMEM((BLOCKS, ER, EC, W), BF),
            pltpu.VMEM((ER, EC, W), F32),
            pltpu.VMEM((3, 32, W), F32),
        ],
        compiler_params=pltpu.CompilerParams(vmem_limit_bytes=56 * MB),
        name="main",
    )(recv, ct, rc, rd, wbig, gains, kern, wht, wl)


def place_kernel(ro, co, recv, out, acc):
    first_row = ro[0] - 1 - LAT_DEV * lax.axis_index("row")
    off = co[0] - 1 - LON_DEV * col_place()
    q = iota((192, 512), 0)
    lane = iota((192, 512), 1)
    h = lane >> 8
    lj = lane & 255
    c = q // 24
    j = q - c * 24 - 10 * h
    sel = one_hot((j >= 0) & (j < 10) & (lj == off + 8 * c + j) & (lj < LON_DEV))
    acc[...] = jnp.zeros_like(acc)

    def row(r, _):
        a = recv[:, r].astype(F32).reshape(192, 128).astype(BF)
        o = dotf(a, sel, TN)
        for k in range(3):
            acc[r + k, :40] = acc[r + k, :40] + o[40 * k : 40 * k + 40, :256]
            acc[r + k, 40:] = acc[r + k, 40:] + o[40 * k : 40 * k + 40, 256:]
        return 0

    lax.fori_loop(0, 16, row, 0)
    out[...] = jnp.zeros_like(out)

    def store(i, _):
        li = first_row + i

        @pl.when((li >= 0) & (li < LAT_DEV))
        def _():
            out[jnp.clip(li, 0, LAT_DEV - 1)] = acc[i, :CIN, :LON_DEV]

        return 0

    lax.fori_loop(0, 18, store, 0)


def place(ro, co, recv):
    return pl.pallas_call(
        place_kernel,
        out_shape=jax.ShapeDtypeStruct((LAT_DEV, CIN, LON_DEV), F32),
        in_specs=[SM, SM, VM],
        out_specs=VM,
        scratch_shapes=[pltpu.VMEM((18, 80, 256), F32)],
        compiler_params=pltpu.CompilerParams(vmem_limit_bytes=32 * MB),
        name="place",
    )(ro, co, recv)


def shards(coarse, ro, co, static, w_lift, w_static, gains, kern, w_head, cot):
    send, xown, pa, pb = pack(ro, co, coarse, static, cot)
    recv = lax.all_to_all(send, ("sec", "row", "col"), 0, 0, tiled=True)
    near = [(i, i ^ 1) for i in range(16)]
    far = [(i, j) for i in range(16) for j in [i + 1 if i & 1 else i - 1] if 0 <= j < 16]
    ra = lax.ppermute(pa, "row", near)
    rb = lax.ppermute(pb, "row", far)
    ct, pc, pd = edges(xown, ra, rb)
    near = [(i, i ^ 1) for i in range(8)]
    far = [(i, j) for i in range(8) for j in [i + 1 if i & 1 else i - 1] if 0 <= j < 8]
    rc = lax.ppermute(pc, ("sec", "col"), near)
    rd = lax.ppermute(pd, ("sec", "col"), far)

    wht = w_head.T
    zero = jnp.zeros
    wbig = jnp.concatenate(
        [
            jnp.concatenate([w_lift, zero((50, W), BF), zero((80, W), BF), w_static, zero((44, W), BF)], 0),
            jnp.concatenate([zero((128, W), BF), wht, zero((50, W), BF)], 0),
        ],
        1,
    )
    wht80 = jnp.concatenate([wht, zero((2, W), BF)], 0)
    wl = jnp.concatenate([w_lift, zero((2, W), BF)], 0).reshape(2, 40, W).transpose(2, 0, 1)
    wl = jnp.concatenate(
        [jnp.pad(wl, ((0, 0), (0, 0), (40 * k, 88 - 40 * k))).reshape(W, 256) for k in range(3)], 0
    )
    fine, msg = main(recv, ct, rc, rd, wbig, gains, kern, wht80, wl)
    back = lax.all_to_all(msg, ("sec", "row", "col"), 0, 0, tiled=True)
    return fine, place(ro, co, back.reshape(2, 16, 4, 24, 128))


def solution(mesh):
    tile = P("row", None, ("sec", "col"))
    in_specs = (tile, P(), P(), tile, P(), P(), P(), P(), P(), tile)
    return jax.shard_map(shards, mesh=mesh, in_specs=in_specs, out_specs=(tile, tile), check_vma=False)
```

```python
import functools

import jax
import jax.numpy as jnp
from jax import lax
from jax.experimental import pallas as pl
from jax.experimental.pallas import tpu as pltpu
from jax.sharding import PartitionSpec as P

R = 16
CIN = 78
W = 256
BLOCKS = 4
TR = 16
TC = 128
LAT_DEV = 45
LON_DEV = 180
HR = 6
HC = 8
ER = TR + 2 * HR
L = 9
S = 16
EC = L * S
BF = jnp.bfloat16
F32 = jnp.float32
VM = pl.BlockSpec(memory_space=pltpu.VMEM)
SM = pl.BlockSpec(memory_space=pltpu.SMEM)
MB = 2**20
NT = (((1,), (1,)), ((), ()))
NN = (((1,), (0,)), ((), ()))
TN = (((0,), (0,)), ((), ()))


def dotf(a, b, dims=NN):
    return lax.dot_general(a, b, dims, preferred_element_type=F32)


def iota(shape, dim):
    return lax.broadcasted_iota(jnp.int32, shape, dim)


def ext_col(m):
    return (m & 15) * L + (m >> 4)


def one_hot(cond):
    return jnp.where(cond, 1.0, 0.0).astype(BF)


def col_weight(e, j):
    n = 2 * e + 1
    a = n >> 5
    t = (n & 31).astype(F32) * (1.0 / 32.0)
    return jnp.where(j == a, 1.0 - t, 0.0) + jnp.where(j == a + 1, t, 0.0)


def col_place():
    return lax.axis_index("sec") * 4 + lax.axis_index("col")


def pack_kernel(ro, co, coarse, static, cot, send, xown, pa, pb, prod):
    ri = lax.axis_index("row")
    ci = col_place()
    first_row = ro[0] - 1 - LAT_DEV * ri
    off = co[0] - 1 - LON_DEV * ci
    lj = iota((272, LON_DEV), 1)
    q = iota((272, LON_DEV), 0)
    tail = q - 80
    k = tail >> 6
    c = (tail & 63) >> 3
    s = (tail & 7) - 2 * k
    j_tail = jnp.where((s >= 0) & (s < 2), 8 * c + 8 + s, -100000)
    j = jnp.where(q < 80, jnp.where(q < 66, q, -100000), j_tail)
    sel = one_hot(lj == off + j)

    def row(i, _):
        li = first_row + i
        ok = ((li >= 0) & (li < LAT_DEV)).astype(F32)
        x = coarse[jnp.clip(li, 0, LAT_DEV - 1)]
        prod[i, :, :CIN] = dotf(sel, x, NT) * ok
        return 0

    lax.fori_loop(0, 18, row, 0)

    def dest(r, _):
        tails = prod[r, 80:144] + prod[r + 1, 144:208] + prod[r + 2, 208:272]
        for cc in range(8):
            d = (cc // 4) * 64 + r * 4 + cc % 4
            sl = slice(8 * cc, 8 * cc + 8)
            msg = jnp.concatenate([prod[r, sl], prod[r + 1, sl], prod[r + 2, sl], tails[sl]], axis=0)
            send[d] = msg.astype(BF)
        return 0

    lax.fori_loop(0, 16, dest, 0)
    xown[...] = jnp.zeros_like(xown)
    xown[:, :CIN, :] = cot[...]
    xown[:, 80:84, :] = static[...]
    odd = ri & 1
    pa[...] = xown[pl.ds(jnp.where(odd == 1, 0, TR - HR), HR)]
    pb[...] = xown[pl.ds(jnp.where(odd == 1, TR - HR, 0), HR)]


def pack(ro, co, coarse, static, cot):
    return pl.pallas_call(
        pack_kernel,
        out_shape=[
            jax.ShapeDtypeStruct((128, 32, 128), BF),
            jax.ShapeDtypeStruct((TR, 128, 128), BF),
            jax.ShapeDtypeStruct((HR, 128, 128), BF),
            jax.ShapeDtypeStruct((HR, 128, 128), BF),
        ],
        in_specs=[SM, SM, VM, VM, VM],
        out_specs=[VM] * 4,
        scratch_shapes=[pltpu.VMEM((18, 272, 128), F32)],
        compiler_params=pltpu.CompilerParams(vmem_limit_bytes=32 * MB),
        name="pack",
    )(ro, co, coarse, static, cot)


def edge_kernel(xown, ra, rb, ct, pc, pd, edge):
    ri = lax.axis_index("row")
    ci = col_place()
    m = iota((EC, 128), 0)
    perm = one_hot(ext_col(m) - HC == iota((EC, 128), 1))
    q = iota((16, 128), 0)
    sel = one_hot(iota((16, 128), 1) == jnp.where(q < 8, q, q + 112))
    both = jnp.concatenate([perm, sel], axis=0)

    def do(y, x):
        r = dotf(both, x, NT)
        ct[y] = r[:EC].astype(BF)
        edge[y] = r[EC:]

    def mid(y, _):
        do(y + HR, xown[y])
        return 0

    lax.fori_loop(0, TR, mid, 0)
    odd = (ri & 1) == 1

    def ends(y, _):
        a = ra[y]
        b = rb[y]
        do(y, jnp.where(odd, a, b))
        do(y + HR + TR, jnp.where(odd, b, a))
        return 0

    lax.fori_loop(0, HR, ends, 0)
    oddc = (ci & 1) == 1
    left = edge[:, :8, :].reshape(ER * 8, 128)
    right = edge[:, 8:, :].reshape(ER * 8, 128)
    pc[...] = jnp.where(oddc, left, right).astype(BF)
    pd[...] = jnp.where(oddc, right, left).astype(BF)


def edges(xown, ra, rb):
    return pl.pallas_call(
        edge_kernel,
        out_shape=[
            jax.ShapeDtypeStruct((ER, EC, 128), BF),
            jax.ShapeDtypeStruct((ER * 8, 128), BF),
            jax.ShapeDtypeStruct((ER * 8, 128), BF),
        ],
        in_specs=[VM] * 3,
        out_specs=[VM] * 3,
        scratch_shapes=[pltpu.VMEM((ER, 16, 128), F32)],
        compiler_params=pltpu.CompilerParams(vmem_limit_bytes=16 * MB),
        name="edges",
    )(xown, ra, rb)


def main_kernel(
    recv, ct, rc, rd, wbig, gains, kern, wht, wl, fine, msg,
    vup, hid, act, cv, hs_s, ds_s, back, gsum,
):
    ri = lax.axis_index("row")
    ci = col_place()
    oddc = (ci & 1) == 1

    win = jnp.sum(recv[...].astype(F32), axis=0)
    win = jnp.where(iota((32, 128), 1) < CIN, win, 0.0).astype(BF)
    m = iota((EC, 32), 0)
    q = iota((EC, 32), 1)
    for k in range(3):
        tail = q - 24 - 2 * k
        j = jnp.where((q >= 8 * k) & (q < 8 * k + 8), q - 8 * k, -10)
        j = jnp.where((tail >= 0) & (tail < 2), tail + 8, j)
        coef = col_weight(ext_col(m), j).astype(BF)
        vup[k] = dotf(coef, win)

    m4 = iota((4 * EC, 32), 0)
    q4 = iota((4 * EC, 32), 1)
    y4 = (
        (m4 >= EC).astype(jnp.int32) + (m4 >= 2 * EC).astype(jnp.int32) + (m4 >= 3 * EC).astype(jnp.int32)
    )
    e4 = ext_col(m4 - y4 * EC)
    same = y4 == (q4 >> 3)
    perm_l = one_hot(same & (e4 == (q4 & 7)))
    perm_r = one_hot(same & (e4 - (HC + TC) == (q4 & 7)))

    def lift(g, _):
        rows = pl.ds(pl.multiple_of(g * 32, 32), 32)
        c = rc[rows, :]
        d = rd[rows, :]
        halo = dotf(perm_l, jnp.where(oddc, c, d)) + dotf(perm_r, jnp.where(oddc, d, c))
        ups = []
        for k in range(4):
            n = 2 * (g * 4 + k) + 5
            a = n >> 5
            t = (n & 31).astype(F32) * (1.0 / 32.0)
            ups.append(((1.0 - t) * vup[a] + t * vup[a + 1]).astype(BF))
        up = jnp.concatenate(ups, axis=0)
        own = ct[pl.ds(g * 4, 4)].reshape(4 * EC, 128)
        both = (own.astype(F32) + halo).astype(BF)
        r = dotf(jnp.concatenate([up, both], axis=1), wbig[...])
        cv[pl.ds(g * 4, 4)] = r[:, :W].reshape(4, EC, W)
        back[pl.ds(g * 4, 4)] = r[:, W:].reshape(4, EC, W)
        return 0

    lax.fori_loop(0, ER // 4, lift, 0)
    hid[...] = jnp.zeros_like(hid)

    CK = 48
    col_ok = []
    for ck in range(3):
        gc = ci * TC + ext_col(iota((CK, 1), 0) + ck * CK) - HC
        col_ok.append(jnp.where((gc >= 0) & (gc < 8 * TC), 1.0, 0.0))

    def put(y, ck, v):
        act[y, 1 + 3 * ck : 4 + 3 * ck] = v.astype(BF).reshape(3, S, W)
        if ck == 2:
            act[y, 0] = pltpu.roll(v[32:48], 1, 0).astype(BF)
        if ck == 0:
            act[y, L + 1] = pltpu.roll(v[:16], S - 1, 0).astype(BF)

    def rows_of(lo, hi, f):
        def two(i, _):
            f(lo + 2 * i)
            f(lo + 2 * i + 1)
            return 0

        lax.fori_loop(0, (hi - lo) >> 1, two, 0)

    def resid(y, ck):
        sl = slice(ck * CK, (ck + 1) * CK)
        h = (hid[y, sl].astype(F32) + cv[y, sl]).astype(BF)
        hid[y, sl] = h
        return h.astype(F32)

    def activate(b, y):
        gr = ri * TR + y - HR
        ok = jnp.where((gr >= 0) & (gr < 16 * TR), 1.0, 0.0)
        gain = gains[pl.ds(b, 1), :]
        for ck in range(3):
            sl = slice(ck * CK, (ck + 1) * CK)
            h = resid(y, ck)
            s = lax.rsqrt(jnp.mean(h * h, axis=-1, keepdims=True) + 1e-06) * (col_ok[ck] * ok)
            hs = h * s
            n = hs * gain
            g = 0.5 * jnp.tanh(0.5 * n) + 0.5
            a = n * g
            put(y, ck, a)
            hs_s[b, y, sl] = hs.astype(BF)
            ds_s[b, y, sl] = ((g + a - a * g) * gain * s).astype(BF)

    def conv(b, lo, hi, transpose):
        dims = NT if transpose else NN

        def unit(i, _):
            y0 = jnp.minimum(lo + 8 * i, hi - 8)

            def rows(k):
                return jnp.concatenate([act[pl.ds(y0 - 1 + k + 2 * u, 1)] for u in range(4)], axis=0)

            d0, d1, d2, d3 = rows(0), rows(1), rows(2), rows(3)
            ms = []
            for k, t in enumerate((d0 - d2, d1 + d2, d2 - d1, d1 - d3)):
                acc = None
                for q in range(3):
                    dx = 2 - q if transpose else q
                    kk = (3, 1, 2, 0)[k] if transpose else k
                    r = dotf(t[:, dx : dx + L].reshape(4 * EC, W), kern[b, kk, q], dims)
                    acc = r if acc is None else acc + r
                ms.append(acc)
            e = (ms[0] + ms[1] + ms[2]).reshape(4, EC, W)
            o = (ms[1] - ms[2] - ms[3]).reshape(4, EC, W)
            for u in range(4):
                cv[y0 + 2 * u] = e[u]
                cv[y0 + 2 * u + 1] = o[u]
            return 0

        lax.fori_loop(0, (hi - lo + 7) >> 3, unit, 0)

    def forward(b, _):
        deep = b == 3
        rows_of(jnp.where(deep, 3, b), jnp.where(deep, ER - 3, ER - b), functools.partial(activate, b))
        conv(b, jnp.where(deep, HR, b + 1), jnp.where(deep, HR + TR, ER - 1 - b), False)
        return 0

    lax.fori_loop(0, BLOCKS, forward, 0)

    def last(y):
        for ck in range(3):
            resid(y, ck)

    rows_of(HR, HR + TR, last)

    perm = one_hot(ext_col(iota((EC, 128), 0)) - HC == iota((EC, 128), 1))

    def head(y, _):
        o = dotf(wht[...], hid[y + HR], NT).astype(BF)
        fine[y] = dotf(o, perm).astype(BF)[:CIN]
        return 0

    lax.fori_loop(0, TR, head, 0)

    def send4(y):
        for ck in range(3):
            put(y, ck, back[y, ck * CK : (ck + 1) * CK, :])

    rows_of(2, ER - 2, send4)

    def grad(b, y):
        for ck in range(3):
            sl = slice(ck * CK, (ck + 1) * CK)
            u = cv[y, sl] * ds_s[b, y, sl].astype(F32)
            hs = hs_s[b, y, sl].astype(F32)
            mean = jnp.mean(u * hs, axis=-1, keepdims=True)
            new = back[y, sl] + (u - hs * mean)
            back[y, sl] = new
            put(y, ck, new)

    def backward(i, _):
        b = 3 - i
        conv(b, HR - b, HR + TR + b, True)
        rows_of(HR - b, HR + TR + b, functools.partial(grad, b))
        return 0

    lax.fori_loop(0, BLOCKS, backward, 0)

    e = ext_col(iota((32, EC), 1))
    qq = iota((32, EC), 0)
    j = jnp.where(qq < 10, qq, jnp.where(qq < 20, qq - 10, -10))
    own = (e >= HC) & (e < HC + TC)
    cols_t = jnp.where(own, col_weight(e, j), 0.0).astype(BF)
    gsum[...] = jnp.zeros_like(gsum)

    def gather(y, _):
        t = dotf(cols_t, back[y + HR].astype(BF))
        n = 2 * (y + HR) + 5
        a = n >> 5
        w = (n & 31).astype(F32) * (1.0 / 32.0)
        gsum[a] = gsum[a] + (1.0 - w) * t
        gsum[a + 1] = gsum[a + 1] + w * t
        return 0

    lax.fori_loop(0, TR, gather, 0)
    g = jnp.concatenate([gsum[0], gsum[1], gsum[2]], axis=1)
    g_hi = g.astype(BF)
    g_lo = (g - g_hi.astype(F32)).astype(BF)
    o = dotf(g_hi, wl[...]) + dotf(g_lo, wl[...])
    o = jnp.where(iota((32, 128), 0) < 10, o[:, :128], o[:, 128:]).astype(BF)[:24]

    def spread(d, _):
        msg[d] = o
        return 0

    lax.fori_loop(0, 128, spread, 0)


def main(recv, ct, rc, rd, wbig, gains, kern, wht, wl):
    return pl.pallas_call(
        main_kernel,
        out_shape=[
            jax.ShapeDtypeStruct((TR, CIN, TC), BF),
            jax.ShapeDtypeStruct((128, 24, 128), BF),
        ],
        in_specs=[VM] * 9,
        out_specs=[VM] * 2,
        scratch_shapes=[
            pltpu.VMEM((3, EC, 128), F32),
            pltpu.VMEM((ER, EC, W), BF),
            pltpu.VMEM((ER, L + 2, S, W), BF),
            pltpu.VMEM((ER, EC, W), F32),
            pltpu.VMEM((BLOCKS, ER, EC, W), BF),
            pltpu.VMEM((BLOCKS, ER, EC, W), BF),
            pltpu.VMEM((ER, EC, W), F32),
            pltpu.VMEM((3, 32, W), F32),
        ],
        compiler_params=pltpu.CompilerParams(vmem_limit_bytes=56 * MB),
        name="main",
    )(recv, ct, rc, rd, wbig, gains, kern, wht, wl)


def place_kernel(ro, co, recv, out, acc):
    first_row = ro[0] - 1 - LAT_DEV * lax.axis_index("row")
    off = co[0] - 1 - LON_DEV * col_place()
    q = iota((192, 512), 0)
    lane = iota((192, 512), 1)
    h = lane >> 8
    lj = lane & 255
    c = q // 24
    j = q - c * 24 - 10 * h
    sel = one_hot((j >= 0) & (j < 10) & (lj == off + 8 * c + j) & (lj < LON_DEV))
    acc[...] = jnp.zeros_like(acc)

    def row(r, _):
        a = recv[:, r].astype(F32).reshape(192, 128).astype(BF)
        o = dotf(a, sel, TN)
        for k in range(3):
            acc[r + k, :40] = acc[r + k, :40] + o[40 * k : 40 * k + 40, :256]
            acc[r + k, 40:] = acc[r + k, 40:] + o[40 * k : 40 * k + 40, 256:]
        return 0

    lax.fori_loop(0, 16, row, 0)
    out[...] = jnp.zeros_like(out)

    def store(i, _):
        li = first_row + i

        @pl.when((li >= 0) & (li < LAT_DEV))
        def _():
            out[jnp.clip(li, 0, LAT_DEV - 1)] = acc[i, :CIN, :LON_DEV]

        return 0

    lax.fori_loop(0, 18, store, 0)


def place(ro, co, recv):
    return pl.pallas_call(
        place_kernel,
        out_shape=jax.ShapeDtypeStruct((LAT_DEV, CIN, LON_DEV), F32),
        in_specs=[SM, SM, VM],
        out_specs=VM,
        scratch_shapes=[pltpu.VMEM((18, 80, 256), F32)],
        compiler_params=pltpu.CompilerParams(vmem_limit_bytes=32 * MB),
        name="place",
    )(ro, co, recv)


def shards(coarse, ro, co, static, w_lift, w_static, gains, kern, w_head, cot):
    send, xown, pa, pb = pack(ro, co, coarse, static, cot)
    recv = lax.all_to_all(send, ("sec", "row", "col"), 0, 0, tiled=True)
    near = [(i, i ^ 1) for i in range(16)]
    far = [(i, j) for i in range(16) for j in [i + 1 if i & 1 else i - 1] if 0 <= j < 16]
    ra = lax.ppermute(pa, "row", near)
    rb = lax.ppermute(pb, "row", far)
    ct, pc, pd = edges(xown, ra, rb)
    near = [(i, i ^ 1) for i in range(8)]
    far = [(i, j) for i in range(8) for j in [i + 1 if i & 1 else i - 1] if 0 <= j < 8]
    rc = lax.ppermute(pc, ("sec", "col"), near)
    rd = lax.ppermute(pd, ("sec", "col"), far)

    wht = w_head.T
    zero = jnp.zeros
    wbig = jnp.concatenate(
        [
            jnp.concatenate([w_lift, zero((50, W), BF), zero((80, W), BF), w_static, zero((44, W), BF)], 0),
            jnp.concatenate([zero((128, W), BF), wht, zero((50, W), BF)], 0),
        ],
        1,
    )
    wht80 = jnp.concatenate([wht, zero((2, W), BF)], 0)
    wl = jnp.concatenate([w_lift, zero((2, W), BF)], 0).reshape(2, 40, W).transpose(2, 0, 1)
    wl = jnp.concatenate(
        [jnp.pad(wl, ((0, 0), (0, 0), (40 * k, 88 - 40 * k))).reshape(W, 256) for k in range(3)], 0
    )
    k0, k1, k2 = (kern[:, p].astype(F32) for p in range(3))
    wino = jnp.stack([k0, 0.5 * (k0 + k1 + k2), 0.5 * (k0 - k1 + k2), k2], axis=1).astype(BF)
    fine, msg = main(recv, ct, rc, rd, wbig, gains, wino, wht80, wl)
    back = lax.all_to_all(msg, ("sec", "row", "col"), 0, 0, tiled=True)
    return fine, place(ro, co, back.reshape(2, 16, 4, 24, 128))


def solution(mesh):
    tile = P("row", None, ("sec", "col"))
    in_specs = (tile, P(), P(), tile, P(), P(), P(), P(), P(), tile)
    return jax.shard_map(shards, mesh=mesh, in_specs=in_specs, out_specs=(tile, tile), check_vma=False)
```

```python
import functools

import jax
import jax.numpy as jnp
from jax import lax
from jax.experimental import pallas as pl
from jax.experimental.pallas import tpu as pltpu
from jax.sharding import PartitionSpec as P

R = 16
CIN = 78
W = 256
BLOCKS = 4
TR = 16
TC = 128
LAT_DEV = 45
LON_DEV = 180
HR = 6
HC = 8
ER = TR + 2 * HR
L = 9
S = 16
EC = L * S
BF = jnp.bfloat16
F32 = jnp.float32
VM = pl.BlockSpec(memory_space=pltpu.VMEM)
SM = pl.BlockSpec(memory_space=pltpu.SMEM)
MB = 2**20
NT = (((1,), (1,)), ((), ()))
NN = (((1,), (0,)), ((), ()))
TN = (((0,), (0,)), ((), ()))


def dotf(a, b, dims=NN):
    return lax.dot_general(a, b, dims, preferred_element_type=F32)


def iota(shape, dim):
    return lax.broadcasted_iota(jnp.int32, shape, dim)


def ext_col(m):
    return (m & 15) * L + (m >> 4)


def one_hot(cond):
    return jnp.where(cond, 1.0, 0.0).astype(BF)


def col_weight(e, j):
    n = 2 * e + 1
    a = n >> 5
    t = (n & 31).astype(F32) * (1.0 / 32.0)
    return jnp.where(j == a, 1.0 - t, 0.0) + jnp.where(j == a + 1, t, 0.0)


def col_place():
    return lax.axis_index("sec") * 4 + lax.axis_index("col")


def rows_kernel(static, cot, xown, pa, pb):
    xown[...] = jnp.zeros_like(xown)
    xown[:, :CIN, :] = cot[...]
    xown[:, 80:84, :] = static[...]
    odd = (lax.axis_index("row") & 1) == 1
    pa[...] = xown[pl.ds(jnp.where(odd, 0, TR - HR), HR)]
    pb[...] = xown[pl.ds(jnp.where(odd, TR - HR, 0), HR)]


def own_rows(static, cot):
    return pl.pallas_call(
        rows_kernel,
        out_shape=[
            jax.ShapeDtypeStruct((TR, 128, 128), BF),
            jax.ShapeDtypeStruct((HR, 128, 128), BF),
            jax.ShapeDtypeStruct((HR, 128, 128), BF),
        ],
        in_specs=[VM] * 2,
        out_specs=[VM] * 3,
        cost_estimate=pl.CostEstimate(flops=0, bytes_accessed=2 * MB, transcendentals=0),
        compiler_params=pltpu.CompilerParams(vmem_limit_bytes=8 * MB),
        name="own_rows",
    )(static, cot)


def pack_kernel(ro, co, coarse, after, send, xs, prod, sem):
    ri = lax.axis_index("row")
    ci = col_place()
    first_row = ro[0] - 1 - LAT_DEV * ri
    off = co[0] - 1 - LON_DEV * ci
    start = jnp.clip(first_row, 0, LAT_DEV - 18)
    copy = pltpu.make_async_copy(coarse.at[pl.ds(start, 18)], xs, sem)
    copy.start()
    lj = iota((272, LON_DEV), 1)
    q = iota((272, LON_DEV), 0)
    tail = q - 80
    k = tail >> 6
    c = (tail & 63) >> 3
    s = (tail & 7) - 2 * k
    j_tail = jnp.where((s >= 0) & (s < 2), 8 * c + 8 + s, -100000)
    j = jnp.where(q < 80, jnp.where(q < 66, q, -100000), j_tail)
    sel = one_hot(lj == off + j)
    copy.wait()

    def rows(g, _):
        for k in range(6):
            i = 6 * g + k
            li = first_row + i
            ok = jnp.where((li >= 0) & (li < LAT_DEV), 1.0, 0.0)
            prod[i, :, :CIN] = dotf(sel, xs[jnp.clip(li - start, 0, 17)], NT) * ok
        return 0

    lax.fori_loop(0, 3, rows, 0)

    def dest(r, _):
        tails = prod[r, 80:144] + prod[r + 1, 144:208] + prod[r + 2, 208:272]
        for cc in range(8):
            d = (cc // 4) * 64 + r * 4 + cc % 4
            sl = slice(8 * cc, 8 * cc + 8)
            msg = jnp.concatenate([prod[r, sl], prod[r + 1, sl], prod[r + 2, sl], tails[sl]], axis=0)
            send[d] = msg.astype(BF)
        return 0

    lax.fori_loop(0, 16, dest, 0)


def pack(ro, co, coarse, after):
    return pl.pallas_call(
        pack_kernel,
        out_shape=jax.ShapeDtypeStruct((128, 32, 128), BF),
        in_specs=[SM, SM, pl.BlockSpec(memory_space=pltpu.HBM), pl.BlockSpec(memory_space=pl.ANY)],
        out_specs=VM,
        scratch_shapes=[
            pltpu.VMEM((18, CIN, LON_DEV), BF),
            pltpu.VMEM((18, 272, 128), F32),
            pltpu.SemaphoreType.DMA(()),
        ],
        cost_estimate=pl.CostEstimate(flops=0, bytes_accessed=8 * MB, transcendentals=0),
        compiler_params=pltpu.CompilerParams(vmem_limit_bytes=16 * MB),
        name="pack",
    )(ro, co, coarse, after)


def edge_kernel(xown, ra, rb, pc, pd, edge):
    odd = (lax.axis_index("row") & 1) == 1
    oddc = (col_place() & 1) == 1
    q = iota((16, 128), 0)
    sel = one_hot(iota((16, 128), 1) == jnp.where(q < 8, q, q + 112))

    def do(y0, x):
        n = x.shape[0]
        r = dotf(sel, x.reshape(n * 128, 128), NT)
        for k in range(n):
            edge[y0 + k] = r[:, k * 128 : (k + 1) * 128]

    do(HR, xown[...])
    a = ra[...]
    b = rb[...]
    do(0, jnp.where(odd, a, b))
    do(HR + TR, jnp.where(odd, b, a))
    left = edge[:, :8, :].reshape(ER * 8, 128)
    right = edge[:, 8:, :].reshape(ER * 8, 128)
    pc[...] = jnp.where(oddc, left, right).astype(BF)
    pd[...] = jnp.where(oddc, right, left).astype(BF)


def edges(xown, ra, rb):
    return pl.pallas_call(
        edge_kernel,
        out_shape=[
            jax.ShapeDtypeStruct((ER * 8, 128), BF),
            jax.ShapeDtypeStruct((ER * 8, 128), BF),
        ],
        in_specs=[VM] * 3,
        out_specs=[VM] * 2,
        scratch_shapes=[pltpu.VMEM((ER, 16, 128), F32)],
        cost_estimate=pl.CostEstimate(flops=0, bytes_accessed=4 * MB, transcendentals=0),
        compiler_params=pltpu.CompilerParams(vmem_limit_bytes=8 * MB),
        name="edges",
    )(xown, ra, rb)


def cells_kernel(xown, ra, rb, rc, rd, ct):
    odd = (lax.axis_index("row") & 1) == 1
    oddc = (col_place() & 1) == 1
    perm = one_hot(ext_col(iota((EC, 128), 0)) - HC == iota((EC, 128), 1))
    m = iota((2 * EC, 16), 0)
    q = iota((2 * EC, 16), 1)
    y2 = (m >= EC).astype(jnp.int32)
    e2 = ext_col(m - y2 * EC)
    same = y2 == (q >> 3)
    perm_l = one_hot(same & (e2 == (q & 7)))
    perm_r = one_hot(same & (e2 - (HC + TC) == (q & 7)))

    def do(y, x):
        rows = pl.ds(pl.multiple_of(y * 8, 16), 16)
        c = rc[rows, :]
        d = rd[rows, :]
        halo = dotf(perm_l, jnp.where(oddc, c, d)) + dotf(perm_r, jnp.where(oddc, d, c))
        for k in range(2):
            ct[y + k] = (dotf(perm, x[k], NT) + halo[k * EC : (k + 1) * EC]).astype(BF)

    def mid(i, _):
        for k in range(2):
            y = 4 * i + 2 * k
            do(y + HR, xown[pl.ds(y, 2)])
        return 0

    lax.fori_loop(0, TR // 4, mid, 0)
    for y in range(0, HR, 2):
        a = ra[y : y + 2]
        b = rb[y : y + 2]
        do(y, jnp.where(odd, a, b))
        do(y + HR + TR, jnp.where(odd, b, a))


def cells(xown, ra, rb, rc, rd):
    return pl.pallas_call(
        cells_kernel,
        out_shape=jax.ShapeDtypeStruct((ER, EC, 128), BF),
        in_specs=[VM] * 5,
        out_specs=VM,
        cost_estimate=pl.CostEstimate(flops=0, bytes_accessed=8 * MB, transcendentals=0),
        compiler_params=pltpu.CompilerParams(vmem_limit_bytes=8 * MB),
        name="cells",
    )(xown, ra, rb, rc, rd)


def pairs_kernel(kern, out):
    k0, k1, k2 = (kern[p].astype(F32) for p in range(3))
    out[0] = kern[0]
    out[1] = (0.5 * (k0 + k1 + k2)).astype(BF)
    out[2] = (0.5 * (k0 - k1 + k2)).astype(BF)
    out[3] = kern[2]


def pairs(kern):
    return pl.pallas_call(
        pairs_kernel,
        out_shape=jax.ShapeDtypeStruct((BLOCKS, 4, 3, W, W), BF),
        grid=(BLOCKS, 3),
        in_specs=[pl.BlockSpec((None, 3, None, W, W), lambda b, q: (b, 0, q, 0, 0))],
        out_specs=pl.BlockSpec((None, 4, None, W, W), lambda b, q: (b, 0, q, 0, 0)),
        cost_estimate=pl.CostEstimate(flops=0, bytes_accessed=12 * MB, transcendentals=0),
        compiler_params=pltpu.CompilerParams(vmem_limit_bytes=8 * MB),
        name="pairs",
    )(kern)


def main_kernel(
    recv, ct, wbig, gains, kern_hbm, wht, wl, fine, msg,
    vup, hid, act, cv, hs_s, ds_s, back, gsum, kern, sem,
):
    ri = lax.axis_index("row")
    ci = col_place()
    load = pltpu.make_async_copy(kern_hbm, kern, sem)
    load.start()

    win = jnp.sum(recv[...].astype(F32), axis=0)
    win = jnp.where(iota((32, 128), 1) < CIN, win, 0.0).astype(BF)
    m = iota((EC, 32), 0)
    q = iota((EC, 32), 1)
    for k in range(3):
        tail = q - 24 - 2 * k
        j = jnp.where((q >= 8 * k) & (q < 8 * k + 8), q - 8 * k, -10)
        j = jnp.where((tail >= 0) & (tail < 2), tail + 8, j)
        coef = col_weight(ext_col(m), j).astype(BF)
        vup[k] = dotf(coef, win)

    def lift(g, _):
        ups = []
        for k in range(4):
            n = 2 * (g * 4 + k) + 5
            a = n >> 5
            t = (n & 31).astype(F32) * (1.0 / 32.0)
            ups.append(((1.0 - t) * vup[a] + t * vup[a + 1]).astype(BF))
        up = jnp.concatenate(ups, axis=0)
        own = ct[pl.ds(g * 4, 4)].reshape(4 * EC, 128)
        r = dotf(jnp.concatenate([up, own], axis=1), wbig[...])
        cv[pl.ds(g * 4, 4)] = r[:, :W].reshape(4, EC, W)
        back[pl.ds(g * 4, 4)] = r[:, W:].reshape(4, EC, W)
        return 0

    lax.fori_loop(0, ER // 4, lift, 0)
    hid[...] = jnp.zeros_like(hid)

    CK = 48
    col_ok = []
    for ck in range(3):
        gc = ci * TC + ext_col(iota((CK, 1), 0) + ck * CK) - HC
        col_ok.append(jnp.where((gc >= 0) & (gc < 8 * TC), 1.0, 0.0))

    def put(y, ck, v):
        act[y, 1 + 3 * ck : 4 + 3 * ck] = v.astype(BF).reshape(3, S, W)
        if ck == 2:
            act[y, 0] = pltpu.roll(v[32:48], 1, 0).astype(BF)
        if ck == 0:
            act[y, L + 1] = pltpu.roll(v[:16], S - 1, 0).astype(BF)

    def rows_of(lo, hi, f):
        def two(i, _):
            f(lo + 2 * i)
            f(lo + 2 * i + 1)
            return 0

        lax.fori_loop(0, (hi - lo) >> 1, two, 0)

    def resid(y, ck):
        sl = slice(ck * CK, (ck + 1) * CK)
        h = (hid[y, sl].astype(F32) + cv[y, sl]).astype(BF)
        hid[y, sl] = h
        return h.astype(F32)

    def activate(b, y):
        gr = ri * TR + y - HR
        ok = jnp.where((gr >= 0) & (gr < 16 * TR), 1.0, 0.0)
        gain = gains[pl.ds(b, 1), :]
        for ck in range(3):
            sl = slice(ck * CK, (ck + 1) * CK)
            h = resid(y, ck)
            s = lax.rsqrt(jnp.mean(h * h, axis=-1, keepdims=True) + 1e-06) * (col_ok[ck] * ok)
            hs = h * s
            n = hs * gain
            g = 0.5 * jnp.tanh(0.5 * n) + 0.5
            a = n * g
            put(y, ck, a)
            hs_s[b, y, sl] = hs.astype(BF)
            ds_s[b, y, sl] = ((g + a - a * g) * gain * s).astype(BF)

    def conv(b, lo, hi, transpose):
        dims = NT if transpose else NN

        def unit(i, _):
            y0 = jnp.minimum(lo + 8 * i, hi - 8)

            def rows(k):
                return jnp.concatenate([act[pl.ds(y0 - 1 + k + 2 * u, 1)] for u in range(4)], axis=0)

            d0, d1, d2, d3 = rows(0), rows(1), rows(2), rows(3)
            ms = []
            for k, t in enumerate((d0 - d2, d1 + d2, d2 - d1, d1 - d3)):
                acc = None
                for q in range(3):
                    dx = 2 - q if transpose else q
                    kk = (3, 1, 2, 0)[k] if transpose else k
                    r = dotf(t[:, dx : dx + L].reshape(4 * EC, W), kern[b, kk, q], dims)
                    acc = r if acc is None else acc + r
                ms.append(acc)
            e = (ms[0] + ms[1] + ms[2]).reshape(4, EC, W)
            o = (ms[1] - ms[2] - ms[3]).reshape(4, EC, W)
            for u in range(4):
                cv[y0 + 2 * u] = e[u]
                cv[y0 + 2 * u + 1] = o[u]
            return 0

        lax.fori_loop(0, (hi - lo + 7) >> 3, unit, 0)

    def forward(b, _):
        deep = b == 3
        rows_of(jnp.where(deep, 3, b), jnp.where(deep, ER - 3, ER - b), functools.partial(activate, b))
        conv(b, jnp.where(deep, HR, b + 1), jnp.where(deep, HR + TR, ER - 1 - b), False)
        return 0

    load.wait()
    lax.fori_loop(0, BLOCKS, forward, 0)

    def last(y):
        for ck in range(3):
            resid(y, ck)

    rows_of(HR, HR + TR, last)

    perm = one_hot(ext_col(iota((EC, 128), 0)) - HC == iota((EC, 128), 1))

    def head(y, _):
        o = dotf(wht[...], hid[y + HR], NT).astype(BF)
        fine[y] = dotf(o, perm).astype(BF)[:CIN]
        return 0

    lax.fori_loop(0, TR, head, 0)

    def send4(y):
        for ck in range(3):
            put(y, ck, back[y, ck * CK : (ck + 1) * CK, :])

    rows_of(2, ER - 2, send4)

    def grad(b, y):
        for ck in range(3):
            sl = slice(ck * CK, (ck + 1) * CK)
            u = cv[y, sl] * ds_s[b, y, sl].astype(F32)
            hs = hs_s[b, y, sl].astype(F32)
            mean = jnp.mean(u * hs, axis=-1, keepdims=True)
            new = back[y, sl] + (u - hs * mean)
            back[y, sl] = new
            put(y, ck, new)

    def backward(i, _):
        b = 3 - i
        conv(b, HR - b, HR + TR + b, True)
        rows_of(HR - b, HR + TR + b, functools.partial(grad, b))
        return 0

    lax.fori_loop(0, BLOCKS, backward, 0)

    e = ext_col(iota((32, EC), 1))
    qq = iota((32, EC), 0)
    j = jnp.where(qq < 10, qq, jnp.where(qq < 20, qq - 10, -10))
    own = (e >= HC) & (e < HC + TC)
    cols_t = jnp.where(own, col_weight(e, j), 0.0).astype(BF)
    gsum[...] = jnp.zeros_like(gsum)

    def gather(y, _):
        t = dotf(cols_t, back[y + HR].astype(BF))
        n = 2 * (y + HR) + 5
        a = n >> 5
        w = (n & 31).astype(F32) * (1.0 / 32.0)
        gsum[a] = gsum[a] + (1.0 - w) * t
        gsum[a + 1] = gsum[a + 1] + w * t
        return 0

    lax.fori_loop(0, TR, gather, 0)
    g = jnp.concatenate([gsum[0], gsum[1], gsum[2]], axis=1)
    g_hi = g.astype(BF)
    g_lo = (g - g_hi.astype(F32)).astype(BF)
    o = dotf(g_hi, wl[...]) + dotf(g_lo, wl[...])
    o = jnp.where(iota((32, 128), 0) < 10, o[:, :128], o[:, 128:]).astype(BF)[:24]

    def spread(d, _):
        msg[d] = o
        return 0

    lax.fori_loop(0, 128, spread, 0)


def main(recv, ct, wbig, gains, kern, wht, wl):
    return pl.pallas_call(
        main_kernel,
        out_shape=[
            jax.ShapeDtypeStruct((TR, CIN, TC), BF),
            jax.ShapeDtypeStruct((128, 24, 128), BF),
        ],
        in_specs=[VM] * 4 + [pl.BlockSpec(memory_space=pltpu.HBM)] + [VM] * 2,
        out_specs=[VM] * 2,
        scratch_shapes=[
            pltpu.VMEM((3, EC, 128), F32),
            pltpu.VMEM((ER, EC, W), BF),
            pltpu.VMEM((ER, L + 2, S, W), BF),
            pltpu.VMEM((ER, EC, W), F32),
            pltpu.VMEM((BLOCKS, ER, EC, W), BF),
            pltpu.VMEM((BLOCKS, ER, EC, W), BF),
            pltpu.VMEM((ER, EC, W), F32),
            pltpu.VMEM((3, 32, W), F32),
            pltpu.VMEM((BLOCKS, 4, 3, W, W), BF),
            pltpu.SemaphoreType.DMA(()),
        ],
        compiler_params=pltpu.CompilerParams(vmem_limit_bytes=58 * MB),
        name="main",
    )(recv, ct, wbig, gains, kern, wht, wl)


def blank_kernel(after, out):
    out[...] = jnp.zeros_like(out)


def blank(after):
    return pl.pallas_call(
        blank_kernel,
        out_shape=jax.ShapeDtypeStruct((LAT_DEV, CIN, LON_DEV), F32),
        grid=(5,),
        in_specs=[pl.BlockSpec(memory_space=pl.ANY)],
        out_specs=pl.BlockSpec((9, CIN, LON_DEV), lambda i: (i, 0, 0)),
        cost_estimate=pl.CostEstimate(flops=0, bytes_accessed=4 * MB, transcendentals=0),
        compiler_params=pltpu.CompilerParams(vmem_limit_bytes=8 * MB),
        name="blank",
    )(after)


def place_kernel(ro, co, recv, zero, out, acc, sem):
    first_row = ro[0] - 1 - LAT_DEV * lax.axis_index("row")
    off = co[0] - 1 - LON_DEV * col_place()
    q = iota((192, 512), 0)
    lane = iota((192, 512), 1)
    h = lane >> 8
    lj = lane & 255
    c = q // 24
    j = q - c * 24 - 10 * h
    sel = one_hot((j >= 0) & (j < 10) & (lj == off + 8 * c + j) & (lj < LON_DEV))
    acc[...] = jnp.zeros_like(acc)

    def rows(g, _):
        for u in range(4):
            r = 4 * g + u
            a = recv[:, r].astype(F32).reshape(192, 128).astype(BF)
            o = dotf(a, sel, TN)
            for k in range(3):
                acc[r + k, :40] = acc[r + k, :40] + o[40 * k : 40 * k + 40, :LON_DEV]
                acc[r + k, 40:] = acc[r + k, 40:] + o[40 * k : 40 * k + 38, 256 : 256 + LON_DEV]
        return 0

    lax.fori_loop(0, 4, rows, 0)
    lo = jnp.clip(-first_row, 0, 18)
    hi = jnp.clip(LAT_DEV - first_row, lo, 18)

    def copy(i):
        li = jnp.clip(first_row + i, 0, LAT_DEV - 1)
        return pltpu.make_async_copy(acc.at[i], out.at[li], sem)

    def start(i, _):
        copy(i).start()
        return 0

    def wait(i, _):
        copy(i).wait()
        return 0

    lax.fori_loop(lo, hi, start, 0)
    lax.fori_loop(lo, hi, wait, 0)


def place(ro, co, recv, zero):
    hbm = pl.BlockSpec(memory_space=pltpu.HBM)
    return pl.pallas_call(
        place_kernel,
        out_shape=jax.ShapeDtypeStruct((LAT_DEV, CIN, LON_DEV), F32),
        in_specs=[SM, SM, VM, hbm],
        out_specs=hbm,
        input_output_aliases={3: 0},
        scratch_shapes=[pltpu.VMEM((18, CIN, LON_DEV), F32), pltpu.SemaphoreType.DMA(())],
        compiler_params=pltpu.CompilerParams(vmem_limit_bytes=16 * MB),
        name="place",
    )(ro, co, recv, zero)


def shards(coarse, ro, co, static, w_lift, w_static, gains, kern, w_head, cot):
    xown, pa, pb = own_rows(static, cot)
    near = [(i, i ^ 1) for i in range(16)]
    far = [(i, j) for i in range(16) for j in [i + 1 if i & 1 else i - 1] if 0 <= j < 16]
    ra = lax.ppermute(pa, "row", near)
    rb = lax.ppermute(pb, "row", far)
    send = pack(ro, co, coarse, pa)
    pc, pd = edges(xown, ra, rb)
    near = [(i, i ^ 1) for i in range(8)]
    far = [(i, j) for i in range(8) for j in [i + 1 if i & 1 else i - 1] if 0 <= j < 8]
    send, pc, pd = lax.optimization_barrier((send, pc, pd))
    rc = lax.ppermute(pc, ("sec", "col"), near)
    rd = lax.ppermute(pd, ("sec", "col"), far)
    recv = lax.all_to_all(send, ("sec", "row", "col"), 0, 0, tiled=True)
    ct = cells(xown, ra, rb, rc, rd)

    wht = w_head.T
    zero = jnp.zeros
    wbig = jnp.concatenate(
        [
            jnp.concatenate([w_lift, zero((50, W), BF), zero((80, W), BF), w_static, zero((44, W), BF)], 0),
            jnp.concatenate([zero((128, W), BF), wht, zero((50, W), BF)], 0),
        ],
        1,
    )
    wht80 = jnp.concatenate([wht, zero((2, W), BF)], 0)
    wl = jnp.concatenate([w_lift, zero((2, W), BF)], 0).reshape(2, 40, W).transpose(2, 0, 1)
    wl = jnp.concatenate(
        [jnp.pad(wl, ((0, 0), (0, 0), (40 * k, 88 - 40 * k))).reshape(W, 256) for k in range(3)], 0
    )
    fine, msg = main(recv, ct, wbig, gains, pairs(kern), wht80, wl)
    back = lax.all_to_all(msg, ("sec", "row", "col"), 0, 0, tiled=True)
    return fine, place(ro, co, back.reshape(2, 16, 4, 24, 128), blank(msg))


def solution(mesh):
    tile = P("row", None, ("sec", "col"))
    in_specs = (tile, P(), P(), tile, P(), P(), P(), P(), P(), tile)
    return jax.shard_map(shards, mesh=mesh, in_specs=in_specs, out_specs=(tile, tile), check_vma=False)
```

```python
import functools

import jax
import jax.numpy as jnp
from jax import lax
from jax.experimental import pallas as pl
from jax.experimental.pallas import tpu as pltpu
from jax.sharding import PartitionSpec as P

R = 16
CIN = 78
W = 256
BLOCKS = 4
TR = 16
TC = 128
LAT_DEV = 45
LON_DEV = 180
HR = 6
HC = 8
ER = TR + 2 * HR
L = 9
S = 16
EC = L * S
BF = jnp.bfloat16
F32 = jnp.float32
VM = pl.BlockSpec(memory_space=pltpu.VMEM)
SM = pl.BlockSpec(memory_space=pltpu.SMEM)
MB = 2**20
NT = (((1,), (1,)), ((), ()))
NN = (((1,), (0,)), ((), ()))
TN = (((0,), (0,)), ((), ()))


def dotf(a, b, dims=NN):
    return lax.dot_general(a, b, dims, preferred_element_type=F32)


def iota(shape, dim):
    return lax.broadcasted_iota(jnp.int32, shape, dim)


def ext_col(m):
    return (m & 15) * L + (m >> 4)


def one_hot(cond):
    return jnp.where(cond, 1.0, 0.0).astype(BF)


def col_weight(e, j):
    n = 2 * e + 1
    a = n >> 5
    t = (n & 31).astype(F32) * (1.0 / 32.0)
    return jnp.where(j == a, 1.0 - t, 0.0) + jnp.where(j == a + 1, t, 0.0)


def col_place():
    return lax.axis_index("sec") * 4 + lax.axis_index("col")


def rows_kernel(static, cot, xown, pa, pb):
    xown[...] = jnp.zeros_like(xown)
    xown[:, :CIN, :] = cot[...]
    xown[:, 80:84, :] = static[...]
    odd = (lax.axis_index("row") & 1) == 1
    pa[...] = xown[pl.ds(jnp.where(odd, 0, TR - HR), HR)]
    pb[...] = xown[pl.ds(jnp.where(odd, TR - HR, 0), HR)]


def own_rows(static, cot):
    return pl.pallas_call(
        rows_kernel,
        out_shape=[
            jax.ShapeDtypeStruct((TR, 128, 128), BF),
            jax.ShapeDtypeStruct((HR, 128, 128), BF),
            jax.ShapeDtypeStruct((HR, 128, 128), BF),
        ],
        in_specs=[VM] * 2,
        out_specs=[VM] * 3,
        cost_estimate=pl.CostEstimate(flops=0, bytes_accessed=2 * MB, transcendentals=0),
        compiler_params=pltpu.CompilerParams(vmem_limit_bytes=8 * MB),
        name="own_rows",
    )(static, cot)


def pack_kernel(ro, co, coarse, after, send, xs, prod, sem):
    ri = lax.axis_index("row")
    ci = col_place()
    first_row = ro[0] - 1 - LAT_DEV * ri
    off = co[0] - 1 - LON_DEV * ci
    start = jnp.clip(first_row, 0, LAT_DEV - 18)
    copy = pltpu.make_async_copy(coarse.at[pl.ds(start, 18)], xs, sem)
    copy.start()
    lj = iota((272, LON_DEV), 1)
    q = iota((272, LON_DEV), 0)
    tail = q - 80
    k = tail >> 6
    c = (tail & 63) >> 3
    s = (tail & 7) - 2 * k
    j_tail = jnp.where((s >= 0) & (s < 2), 8 * c + 8 + s, -100000)
    j = jnp.where(q < 80, jnp.where(q < 66, q, -100000), j_tail)
    sel = one_hot(lj == off + j)
    copy.wait()

    def rows(g, _):
        for k in range(6):
            i = 6 * g + k
            li = first_row + i
            ok = jnp.where((li >= 0) & (li < LAT_DEV), 1.0, 0.0)
            prod[i, :, :CIN] = dotf(sel, xs[jnp.clip(li - start, 0, 17)], NT) * ok
        return 0

    lax.fori_loop(0, 3, rows, 0)

    def dest(r, _):
        tails = prod[r, 80:144] + prod[r + 1, 144:208] + prod[r + 2, 208:272]
        for cc in range(8):
            d = (cc // 4) * 64 + r * 4 + cc % 4
            sl = slice(8 * cc, 8 * cc + 8)
            msg = jnp.concatenate([prod[r, sl], prod[r + 1, sl], prod[r + 2, sl], tails[sl]], axis=0)
            send[d] = msg.astype(BF)
        return 0

    lax.fori_loop(0, 16, dest, 0)


def pack(ro, co, coarse, after):
    return pl.pallas_call(
        pack_kernel,
        out_shape=jax.ShapeDtypeStruct((128, 32, 128), BF),
        in_specs=[SM, SM, pl.BlockSpec(memory_space=pltpu.HBM), pl.BlockSpec(memory_space=pl.ANY)],
        out_specs=VM,
        scratch_shapes=[
            pltpu.VMEM((18, CIN, LON_DEV), BF),
            pltpu.VMEM((18, 272, 128), F32),
            pltpu.SemaphoreType.DMA(()),
        ],
        cost_estimate=pl.CostEstimate(flops=0, bytes_accessed=8 * MB, transcendentals=0),
        compiler_params=pltpu.CompilerParams(vmem_limit_bytes=16 * MB),
        name="pack",
    )(ro, co, coarse, after)


def edge_kernel(xown, ra, rb, pc, pd, edge):
    odd = (lax.axis_index("row") & 1) == 1
    oddc = (col_place() & 1) == 1
    q = iota((16, 128), 0)
    sel = one_hot(iota((16, 128), 1) == jnp.where(q < 8, q, q + 112))

    def do(y0, x):
        n = x.shape[0]
        r = dotf(sel, x.reshape(n * 128, 128), NT)
        for k in range(n):
            edge[y0 + k] = r[:, k * 128 : (k + 1) * 128]

    do(HR, xown[...])
    a = ra[...]
    b = rb[...]
    do(0, jnp.where(odd, a, b))
    do(HR + TR, jnp.where(odd, b, a))
    left = edge[:, :8, :].reshape(ER * 8, 128)
    right = edge[:, 8:, :].reshape(ER * 8, 128)
    pc[...] = jnp.where(oddc, left, right).astype(BF)
    pd[...] = jnp.where(oddc, right, left).astype(BF)


def edges(xown, ra, rb):
    return pl.pallas_call(
        edge_kernel,
        out_shape=[
            jax.ShapeDtypeStruct((ER * 8, 128), BF),
            jax.ShapeDtypeStruct((ER * 8, 128), BF),
        ],
        in_specs=[VM] * 3,
        out_specs=[VM] * 2,
        scratch_shapes=[pltpu.VMEM((ER, 16, 128), F32)],
        cost_estimate=pl.CostEstimate(flops=0, bytes_accessed=4 * MB, transcendentals=0),
        compiler_params=pltpu.CompilerParams(vmem_limit_bytes=8 * MB),
        name="edges",
    )(xown, ra, rb)


def cells_kernel(xown, ra, rb, rc, rd, ct):
    odd = (lax.axis_index("row") & 1) == 1
    oddc = (col_place() & 1) == 1
    perm = one_hot(ext_col(iota((EC, 128), 0)) - HC == iota((EC, 128), 1))
    m = iota((2 * EC, 16), 0)
    q = iota((2 * EC, 16), 1)
    y2 = (m >= EC).astype(jnp.int32)
    e2 = ext_col(m - y2 * EC)
    same = y2 == (q >> 3)
    perm_l = one_hot(same & (e2 == (q & 7)))
    perm_r = one_hot(same & (e2 - (HC + TC) == (q & 7)))

    def do(y, x):
        rows = pl.ds(pl.multiple_of(y * 8, 16), 16)
        c = rc[rows, :]
        d = rd[rows, :]
        halo = dotf(perm_l, jnp.where(oddc, c, d)) + dotf(perm_r, jnp.where(oddc, d, c))
        for k in range(2):
            ct[y + k] = (dotf(perm, x[k], NT) + halo[k * EC : (k + 1) * EC]).astype(BF)

    def mid(i, _):
        for k in range(2):
            y = 4 * i + 2 * k
            do(y + HR, xown[pl.ds(y, 2)])
        return 0

    lax.fori_loop(0, TR // 4, mid, 0)
    for y in range(0, HR, 2):
        a = ra[y : y + 2]
        b = rb[y : y + 2]
        do(y, jnp.where(odd, a, b))
        do(y + HR + TR, jnp.where(odd, b, a))


def cells(xown, ra, rb, rc, rd):
    return pl.pallas_call(
        cells_kernel,
        out_shape=jax.ShapeDtypeStruct((ER, EC, 128), BF),
        in_specs=[VM] * 5,
        out_specs=VM,
        cost_estimate=pl.CostEstimate(flops=0, bytes_accessed=8 * MB, transcendentals=0),
        compiler_params=pltpu.CompilerParams(vmem_limit_bytes=8 * MB),
        name="cells",
    )(xown, ra, rb, rc, rd)


def pairs_kernel(kern, out):
    k0, k1, k2 = (kern[p].astype(F32) for p in range(3))
    out[0] = kern[0]
    out[1] = (0.5 * (k0 + k1 + k2)).astype(BF)
    out[2] = (0.5 * (k0 - k1 + k2)).astype(BF)
    out[3] = kern[2]


def pairs(kern):
    return pl.pallas_call(
        pairs_kernel,
        out_shape=jax.ShapeDtypeStruct((BLOCKS, 4, 3, W, W), BF),
        grid=(BLOCKS, 3),
        in_specs=[pl.BlockSpec((None, 3, None, W, W), lambda b, q: (b, 0, q, 0, 0))],
        out_specs=pl.BlockSpec((None, 4, None, W, W), lambda b, q: (b, 0, q, 0, 0)),
        cost_estimate=pl.CostEstimate(flops=0, bytes_accessed=12 * MB, transcendentals=0),
        compiler_params=pltpu.CompilerParams(vmem_limit_bytes=8 * MB),
        name="pairs",
    )(kern)


def main_kernel(
    recv, ct, wbig, gains, kern_hbm, wht, wl, fine, msg,
    vup, hid_a, hid_b, act_a, act_b, act_c, cv, hs_s, ds_s, gsum, kern, sem,
):
    ri = lax.axis_index("row")
    ci = col_place()
    load = pltpu.make_async_copy(kern_hbm, kern, sem)
    load.start()

    win = jnp.sum(recv[...].astype(F32), axis=0)
    win = jnp.where(iota((32, 128), 1) < CIN, win, 0.0).astype(BF)
    m = iota((EC, 32), 0)
    q = iota((EC, 32), 1)
    for k in range(3):
        tail = q - 24 - 2 * k
        j = jnp.where((q >= 8 * k) & (q < 8 * k + 8), q - 8 * k, -10)
        j = jnp.where((tail >= 0) & (tail < 2), tail + 8, j)
        coef = col_weight(ext_col(m), j).astype(BF)
        vup[k] = dotf(coef, win)

    CK = 48
    col_ok = []
    for ck in range(3):
        gc = ci * TC + ext_col(iota((CK, 1), 0) + ck * CK) - HC
        col_ok.append(jnp.where((gc >= 0) & (gc < 8 * TC), 1.0, 0.0))

    def put(act, y, ck, v):
        act[y, 1 + 3 * ck : 4 + 3 * ck] = v.reshape(3, S, W)
        if ck == 2:
            act[y, 0] = pltpu.roll(v[32:48].astype(F32), 1, 0).astype(BF)
        if ck == 0:
            act[y, L + 1] = pltpu.roll(v[:16].astype(F32), S - 1, 0).astype(BF)

    def lane_mean(v):
        half = (v[:, :128] + v[:, 128:]).astype(F32)
        return jnp.sum(half, axis=-1, keepdims=True) * (1.0 / W)

    def over_lanes(v):
        half = jnp.broadcast_to(v, (v.shape[0], 128)).astype(BF)
        return jnp.concatenate([half, half], axis=1)

    def activate(b, y, ck, before, after, act):
        gr = ri * TR + y - HR
        ok = jnp.where((gr >= 0) & (gr < 16 * TR), 1.0, 0.0)
        gain = gains[pl.ds(jnp.minimum(b, BLOCKS - 1), 1), :].astype(BF)
        keep = jnp.clip(y - 3, 0, 21)
        sl = slice(ck * CK, (ck + 1) * CK)
        h = cv[y, sl]
        if before is not None:
            h = h + before[y, sl]
        after[y, sl] = h
        s = over_lanes(lax.rsqrt(lane_mean(h * h) + 1e-06) * (col_ok[ck] * ok))
        hs = h * s
        n = hs * gain
        half = BF(0.5)
        g = half * jnp.tanh(half * n) + half
        a = n * g
        put(act, y, ck, a)
        hs_s[b, keep, sl] = hs
        ds_s[b, keep, sl] = (g + a - a * g) * (gain * s)

    def lift(g):
        ups = []
        for k in range(4):
            n = 2 * (g * 4 + k) + 5
            a = n >> 5
            t = (n & 31).astype(F32) * (1.0 / 32.0)
            ups.append(((1.0 - t) * vup[a] + t * vup[a + 1]).astype(BF))
        up = jnp.concatenate(ups, axis=0)
        own = ct[pl.ds(g * 4, 4)].reshape(4 * EC, 128)
        r = dotf(jnp.concatenate([up, own], axis=1), wbig[...])
        r = r.astype(BF)
        cv[pl.ds(g * 4, 4)] = r[:, :W].reshape(4, EC, W)
        for k in range(4):
            for ck in range(3):
                put(act_c, g * 4 + k, ck, r[k * EC + ck * CK : k * EC + (ck + 1) * CK, W:])

    def start4(g):
        for k in range(4):
            for ck in range(3):
                activate(0, g * 4 + k, ck, None, hid_a, act_a)

    def lift_on(g, _):
        start4(g - 1)
        lift(jnp.minimum(g, ER // 4 - 1))
        return 0

    lift(jnp.int32(0))
    lax.fori_loop(1, ER // 4 + 1, lift_on, 0)

    def conv(b, act, y0, transpose, between=()):
        between = list(between)
        dims = NT if transpose else NN

        def rows(k):
            return jnp.concatenate([act[pl.ds(y0 - 1 + k + 2 * u, 1)] for u in range(4)], axis=0)

        d0, d1, d2, d3 = rows(0), rows(1), rows(2), rows(3)
        ms = []
        for k, t in enumerate((d0 - d2, d1 + d2, d2 - d1, d1 - d3)):
            acc = None
            for q in range(3):
                dx = 2 - q if transpose else q
                kk = (3, 1, 2, 0)[k] if transpose else k
                r = dotf(t[:, dx : dx + L].reshape(4 * EC, W), kern[b, kk, q], dims)
                acc = r if acc is None else acc + r
                for job in between[:2]:
                    job()
                between = between[2:]
            ms.append(acc)
        e = (ms[0] + ms[1] + ms[2]).reshape(4, EC, W)
        o = (ms[1] - ms[2] - ms[3]).reshape(4, EC, W)
        for u in range(4):
            cv[y0 + 2 * u] = e[u].astype(BF)
            cv[y0 + 2 * u + 1] = o[u].astype(BF)

    def layer(b, lo, hi, act, transpose, after):
        def place(i):
            return jnp.minimum(lo + 8 * i, hi - 8)

        def rest(i):
            y0 = place(i)
            return [functools.partial(after, y0 + k, ck) for k in range(8) for ck in range(3)]

        def unit(i, _):
            conv(b, act, place(i), transpose, rest(i - 1))
            return 0

        n = (hi - lo + 7) >> 3
        conv(b, act, place(0), transpose)
        lax.fori_loop(1, n, unit, 0)
        for job in rest(n - 1):
            job()

    load.wait()

    def forward(i, _):
        for b, src, dst in ((2 * i, (hid_a, act_a), (hid_b, act_b)), (2 * i + 1, (hid_b, act_b), (hid_a, act_a))):
            deep = b == 3
            lo = jnp.where(deep, HR, b + 1)
            hi = jnp.where(deep, HR + TR, ER - 1 - b)

            def after(y, ck, b=b, src=src, dst=dst):
                activate(b + 1, y, ck, src[0], *dst)

            layer(b, lo, hi, src[1], False, after)
        return 0

    lax.fori_loop(0, 2, forward, 0)

    perm = one_hot(ext_col(iota((EC, 128), 0)) - HC == iota((EC, 128), 1))

    def head(g, _):
        for k in range(4):
            y = 4 * g + k
            o = dotf(wht[...], hid_a[y + HR], NT).astype(BF)
            fine[y] = dotf(o, perm).astype(BF)[:CIN]
        return 0

    lax.fori_loop(0, TR // 4, head, 0)

    def grad(b, y, ck, before, act):
        sl = slice(ck * CK, (ck + 1) * CK)
        u = cv[y, sl] * ds_s[b, y - 3, sl]
        hs = hs_s[b, y - 3, sl]
        old = before[y, 1 + 3 * ck : 4 + 3 * ck].reshape(CK, W)
        put(act, y, ck, old + (u - hs * over_lanes(lane_mean(u * hs))))

    def backward(i, _):
        for b, src, dst in ((3 - 2 * i, act_c, act_a), (2 - 2 * i, act_a, act_c)):

            def after(y, ck, b=b, src=src, dst=dst):
                grad(b, y, ck, src, dst)

            layer(b, HR - b, HR + TR + b, src, True, after)
        return 0

    lax.fori_loop(0, 2, backward, 0)

    e = ext_col(iota((32, EC), 1))
    qq = iota((32, EC), 0)
    j = jnp.where(qq < 10, qq, jnp.where(qq < 20, qq - 10, -10))
    own = (e >= HC) & (e < HC + TC)
    cols_t = jnp.where(own, col_weight(e, j), 0.0).astype(BF)
    gsum[...] = jnp.zeros_like(gsum)

    def gather(g, _):
        for k in range(4):
            y = 4 * g + k + HR
            t = dotf(cols_t, act_c[y, 1 : 1 + L].reshape(EC, W))
            n = 2 * y + 5
            a = n >> 5
            w = (n & 31).astype(F32) * (1.0 / 32.0)
            gsum[a] = gsum[a] + (1.0 - w) * t
            gsum[a + 1] = gsum[a + 1] + w * t
        return 0

    lax.fori_loop(0, TR // 4, gather, 0)
    g = jnp.concatenate([gsum[0], gsum[1], gsum[2]], axis=1)
    g_hi = g.astype(BF)
    g_lo = (g - g_hi.astype(F32)).astype(BF)
    o = dotf(g_hi, wl[...]) + dotf(g_lo, wl[...])
    o = jnp.where(iota((32, 128), 0) < 10, o[:, :128], o[:, 128:]).astype(BF)[:24]

    def spread(d, _):
        msg[d] = o
        return 0

    lax.fori_loop(0, 128, spread, 0)


def main(recv, ct, wbig, gains, kern, wht, wl):
    return pl.pallas_call(
        main_kernel,
        out_shape=[
            jax.ShapeDtypeStruct((TR, CIN, TC), BF),
            jax.ShapeDtypeStruct((128, 24, 128), BF),
        ],
        in_specs=[VM] * 4 + [pl.BlockSpec(memory_space=pltpu.HBM)] + [VM] * 2,
        out_specs=[VM] * 2,
        scratch_shapes=[
            pltpu.VMEM((3, EC, 128), F32),
            pltpu.VMEM((ER, EC, W), BF),
            pltpu.VMEM((ER, EC, W), BF),
            pltpu.VMEM((ER, L + 2, S, W), BF),
            pltpu.VMEM((ER, L + 2, S, W), BF),
            pltpu.VMEM((ER, L + 2, S, W), BF),
            pltpu.VMEM((ER, EC, W), BF),
            pltpu.VMEM((BLOCKS + 1, ER - 6, EC, W), BF),
            pltpu.VMEM((BLOCKS + 1, ER - 6, EC, W), BF),
            pltpu.VMEM((3, 32, W), F32),
            pltpu.VMEM((BLOCKS, 4, 3, W, W), BF),
            pltpu.SemaphoreType.DMA(()),
        ],
        compiler_params=pltpu.CompilerParams(vmem_limit_bytes=58 * MB),
        name="main",
    )(recv, ct, wbig, gains, kern, wht, wl)


def blank_kernel(after, out):
    out[...] = jnp.zeros_like(out)


def blank(after):
    return pl.pallas_call(
        blank_kernel,
        out_shape=jax.ShapeDtypeStruct((LAT_DEV, CIN, LON_DEV), F32),
        grid=(5,),
        in_specs=[pl.BlockSpec(memory_space=pl.ANY)],
        out_specs=pl.BlockSpec((9, CIN, LON_DEV), lambda i: (i, 0, 0)),
        cost_estimate=pl.CostEstimate(flops=0, bytes_accessed=4 * MB, transcendentals=0),
        compiler_params=pltpu.CompilerParams(vmem_limit_bytes=8 * MB),
        name="blank",
    )(after)


def place_kernel(ro, co, recv, zero, out, acc, sem):
    first_row = ro[0] - 1 - LAT_DEV * lax.axis_index("row")
    off = co[0] - 1 - LON_DEV * col_place()
    q = iota((192, 512), 0)
    lane = iota((192, 512), 1)
    h = lane >> 8
    lj = lane & 255
    c = q // 24
    j = q - c * 24 - 10 * h
    sel = one_hot((j >= 0) & (j < 10) & (lj == off + 8 * c + j) & (lj < LON_DEV))
    acc[...] = jnp.zeros_like(acc)

    def rows(g, _):
        for u in range(4):
            r = 4 * g + u
            a = recv[:, r].astype(F32).reshape(192, 128).astype(BF)
            o = dotf(a, sel, TN)
            for k in range(3):
                acc[r + k, :40] = acc[r + k, :40] + o[40 * k : 40 * k + 40, :LON_DEV]
                acc[r + k, 40:] = acc[r + k, 40:] + o[40 * k : 40 * k + 38, 256 : 256 + LON_DEV]
        return 0

    lax.fori_loop(0, 4, rows, 0)
    lo = jnp.clip(-first_row, 0, 18)
    hi = jnp.clip(LAT_DEV - first_row, lo, 18)

    def copy(i):
        li = jnp.clip(first_row + i, 0, LAT_DEV - 1)
        return pltpu.make_async_copy(acc.at[i], out.at[li], sem)

    def start(i, _):
        copy(i).start()
        return 0

    def wait(i, _):
        copy(i).wait()
        return 0

    lax.fori_loop(lo, hi, start, 0)
    lax.fori_loop(lo, hi, wait, 0)


def place(ro, co, recv, zero):
    hbm = pl.BlockSpec(memory_space=pltpu.HBM)
    return pl.pallas_call(
        place_kernel,
        out_shape=jax.ShapeDtypeStruct((LAT_DEV, CIN, LON_DEV), F32),
        in_specs=[SM, SM, VM, hbm],
        out_specs=hbm,
        input_output_aliases={3: 0},
        scratch_shapes=[pltpu.VMEM((18, CIN, LON_DEV), F32), pltpu.SemaphoreType.DMA(())],
        compiler_params=pltpu.CompilerParams(vmem_limit_bytes=16 * MB),
        name="place",
    )(ro, co, recv, zero)


def shards(coarse, ro, co, static, w_lift, w_static, gains, kern, w_head, cot):
    xown, pa, pb = own_rows(static, cot)
    near = [(i, i ^ 1) for i in range(16)]
    far = [(i, j) for i in range(16) for j in [i + 1 if i & 1 else i - 1] if 0 <= j < 16]
    ra = lax.ppermute(pa, "row", near)
    rb = lax.ppermute(pb, "row", far)
    send = pack(ro, co, coarse, pa)
    pc, pd = edges(xown, ra, rb)
    near = [(i, i ^ 1) for i in range(8)]
    far = [(i, j) for i in range(8) for j in [i + 1 if i & 1 else i - 1] if 0 <= j < 8]
    send, pc, pd = lax.optimization_barrier((send, pc, pd))
    rc = lax.ppermute(pc, ("sec", "col"), near)
    rd = lax.ppermute(pd, ("sec", "col"), far)
    recv = lax.all_to_all(send, ("sec", "row", "col"), 0, 0, tiled=True)
    ct = cells(xown, ra, rb, rc, rd)

    wht = w_head.T
    zero = jnp.zeros
    wbig = jnp.concatenate(
        [
            jnp.concatenate([w_lift, zero((50, W), BF), zero((80, W), BF), w_static, zero((44, W), BF)], 0),
            jnp.concatenate([zero((128, W), BF), wht, zero((50, W), BF)], 0),
        ],
        1,
    )
    wht80 = jnp.concatenate([wht, zero((2, W), BF)], 0)
    wl = jnp.concatenate([w_lift, zero((2, W), BF)], 0).reshape(2, 40, W).transpose(2, 0, 1)
    wl = jnp.concatenate(
        [jnp.pad(wl, ((0, 0), (0, 0), (40 * k, 88 - 40 * k))).reshape(W, 256) for k in range(3)], 0
    )
    fine, msg = main(recv, ct, wbig, gains, pairs(kern), wht80, wl)
    back = lax.all_to_all(msg, ("sec", "row", "col"), 0, 0, tiled=True)
    return fine, place(ro, co, back.reshape(2, 16, 4, 24, 128), blank(msg))


def solution(mesh):
    tile = P("row", None, ("sec", "col"))
    in_specs = (tile, P(), P(), tile, P(), P(), P(), P(), P(), tile)
    return jax.shard_map(shards, mesh=mesh, in_specs=in_specs, out_specs=(tile, tile), check_vma=False)
```

```python
import functools

import jax
import jax.numpy as jnp
from jax import lax
from jax.experimental import pallas as pl
from jax.experimental.pallas import tpu as pltpu
from jax.sharding import PartitionSpec as P

R = 16
CIN = 78
W = 256
BLOCKS = 4
TR = 16
TC = 128
LAT_DEV = 45
LON_DEV = 180
HR = 6
HC = 8
ER = TR + 2 * HR
L = 9
S = 16
EC = L * S
BF = jnp.bfloat16
F32 = jnp.float32
VM = pl.BlockSpec(memory_space=pltpu.VMEM)
SM = pl.BlockSpec(memory_space=pltpu.SMEM)
MB = 2**20
NT = (((1,), (1,)), ((), ()))
NN = (((1,), (0,)), ((), ()))
TN = (((0,), (0,)), ((), ()))


def dotf(a, b, dims=NN):
    return lax.dot_general(a, b, dims, preferred_element_type=F32)


def iota(shape, dim):
    return lax.broadcasted_iota(jnp.int32, shape, dim)


def ext_col(m):
    return (m & 15) * L + (m >> 4)


def one_hot(cond):
    return jnp.where(cond, 1.0, 0.0).astype(BF)


def col_weight(e, j):
    n = 2 * e + 1
    a = n >> 5
    t = (n & 31).astype(F32) * (1.0 / 32.0)
    return jnp.where(j == a, 1.0 - t, 0.0) + jnp.where(j == a + 1, t, 0.0)


def col_place():
    return lax.axis_index("sec") * 4 + lax.axis_index("col")


def rows_kernel(static, cot, xown, pa, pb):
    xown[...] = jnp.zeros_like(xown)
    xown[:, :CIN, :] = cot[...]
    xown[:, 80:84, :] = static[...]
    odd = (lax.axis_index("row") & 1) == 1
    pa[...] = xown[pl.ds(jnp.where(odd, 0, TR - HR), HR)]
    pb[...] = xown[pl.ds(jnp.where(odd, TR - HR, 0), HR)]


def own_rows(static, cot):
    return pl.pallas_call(
        rows_kernel,
        out_shape=[
            jax.ShapeDtypeStruct((TR, 128, 128), BF),
            jax.ShapeDtypeStruct((HR, 128, 128), BF),
            jax.ShapeDtypeStruct((HR, 128, 128), BF),
        ],
        in_specs=[VM] * 2,
        out_specs=[VM] * 3,
        cost_estimate=pl.CostEstimate(flops=0, bytes_accessed=2 * MB, transcendentals=0),
        compiler_params=pltpu.CompilerParams(vmem_limit_bytes=8 * MB),
        name="own_rows",
    )(static, cot)


def pack_kernel(ro, co, coarse, after, send, xs, prod, sem):
    ri = lax.axis_index("row")
    ci = col_place()
    first_row = ro[0] - 1 - LAT_DEV * ri
    off = co[0] - 1 - LON_DEV * ci
    start = jnp.clip(first_row, 0, LAT_DEV - 18)
    copy = pltpu.make_async_copy(coarse.at[pl.ds(start, 18)], xs, sem)
    copy.start()
    lj = iota((144, LON_DEV), 1)
    q = iota((144, LON_DEV), 0)
    tail = q - 80
    j_tail = jnp.where((tail & 7) < 4, 8 * (tail >> 3) + 8 + (tail & 1), -100000)
    j = jnp.where(q < 80, jnp.where(q < 66, q, -100000), j_tail)
    sel = one_hot(lj == off + j)
    prod[...] = jnp.zeros_like(prod)
    copy.wait()

    def rows(g, _):
        for k in range(6):
            i = 6 * g + k
            li = first_row + i
            ok = jnp.where((li >= 0) & (li < LAT_DEV), 1.0, 0.0)
            prod[i, :, :CIN] = dotf(sel, xs[jnp.clip(li - start, 0, 17)], NT) * ok
        return 0

    lax.fori_loop(0, 3, rows, 0)
    lane = iota((144, 128), 1)
    is_0 = lane < 40
    is_1 = lane < 80
    low = iota((64, 128), 0)
    low = (low & 7) < 2

    def dest(r, _):
        p0 = prod[r]
        p1 = prod[r + 1]
        p2 = prod[r + 2]
        up = pltpu.roll(p1, 40, 1)
        m0 = jnp.where(is_0, p0, jnp.where(is_1, up, pltpu.roll(p2, 80, 1)))
        m1 = jnp.where(is_0, pltpu.roll(p0, 88, 1), jnp.where(is_1, p1, pltpu.roll(p2, 40, 1)))
        tails = jnp.where(low, m0[80:], m1[80:])
        for cc in range(8):
            d = (cc // 4) * 64 + r * 4 + cc % 4
            sl = slice(8 * cc, 8 * cc + 8)
            send[d] = jnp.concatenate([m0[sl], m1[sl], tails[sl]], axis=0).astype(BF)
        return 0

    lax.fori_loop(0, 16, dest, 0)


def pack(ro, co, coarse, after):
    return pl.pallas_call(
        pack_kernel,
        out_shape=jax.ShapeDtypeStruct((128, 24, 128), BF),
        in_specs=[SM, SM, pl.BlockSpec(memory_space=pltpu.HBM), pl.BlockSpec(memory_space=pl.ANY)],
        out_specs=VM,
        scratch_shapes=[
            pltpu.VMEM((18, CIN, LON_DEV), BF),
            pltpu.VMEM((18, 144, 128), F32),
            pltpu.SemaphoreType.DMA(()),
        ],
        cost_estimate=pl.CostEstimate(flops=0, bytes_accessed=8 * MB, transcendentals=0),
        compiler_params=pltpu.CompilerParams(vmem_limit_bytes=16 * MB),
        name="pack",
    )(ro, co, coarse, after)


def edge_kernel(xown, ra, rb, pc, pd, edge):
    odd = (lax.axis_index("row") & 1) == 1
    oddc = (col_place() & 1) == 1
    q = iota((16, 128), 0)
    sel = one_hot(iota((16, 128), 1) == jnp.where(q < 8, q, q + 112))

    def do(y0, x):
        n = x.shape[0]
        r = dotf(sel, x.reshape(n * 128, 128), NT)
        for k in range(n):
            edge[y0 + k] = r[:, k * 128 : (k + 1) * 128]

    do(HR, xown[...])
    a = ra[...]
    b = rb[...]
    do(0, jnp.where(odd, a, b))
    do(HR + TR, jnp.where(odd, b, a))
    left = edge[:, :8, :].reshape(ER * 8, 128)
    right = edge[:, 8:, :].reshape(ER * 8, 128)
    pc[...] = jnp.where(oddc, left, right).astype(BF)
    pd[...] = jnp.where(oddc, right, left).astype(BF)


def edges(xown, ra, rb):
    return pl.pallas_call(
        edge_kernel,
        out_shape=[
            jax.ShapeDtypeStruct((ER * 8, 128), BF),
            jax.ShapeDtypeStruct((ER * 8, 128), BF),
        ],
        in_specs=[VM] * 3,
        out_specs=[VM] * 2,
        scratch_shapes=[pltpu.VMEM((ER, 16, 128), F32)],
        cost_estimate=pl.CostEstimate(flops=0, bytes_accessed=4 * MB, transcendentals=0),
        compiler_params=pltpu.CompilerParams(vmem_limit_bytes=8 * MB),
        name="edges",
    )(xown, ra, rb)


def cells_kernel(xown, ra, rb, rc, rd, ct):
    odd = (lax.axis_index("row") & 1) == 1
    oddc = (col_place() & 1) == 1
    perm = one_hot(ext_col(iota((EC, 128), 0)) - HC == iota((EC, 128), 1))
    m = iota((2 * EC, 16), 0)
    q = iota((2 * EC, 16), 1)
    y2 = (m >= EC).astype(jnp.int32)
    e2 = ext_col(m - y2 * EC)
    same = y2 == (q >> 3)
    perm_l = one_hot(same & (e2 == (q & 7)))
    perm_r = one_hot(same & (e2 - (HC + TC) == (q & 7)))

    def do(y, x):
        rows = pl.ds(pl.multiple_of(y * 8, 16), 16)
        c = rc[rows, :]
        d = rd[rows, :]
        halo = dotf(perm_l, jnp.where(oddc, c, d)) + dotf(perm_r, jnp.where(oddc, d, c))
        for k in range(2):
            ct[y + k] = (dotf(perm, x[k], NT) + halo[k * EC : (k + 1) * EC]).astype(BF)

    def mid(i, _):
        for k in range(2):
            y = 4 * i + 2 * k
            do(y + HR, xown[pl.ds(y, 2)])
        return 0

    lax.fori_loop(0, TR // 4, mid, 0)
    for y in range(0, HR, 2):
        a = ra[y : y + 2]
        b = rb[y : y + 2]
        do(y, jnp.where(odd, a, b))
        do(y + HR + TR, jnp.where(odd, b, a))


def cells(xown, ra, rb, rc, rd):
    return pl.pallas_call(
        cells_kernel,
        out_shape=jax.ShapeDtypeStruct((ER, EC, 128), BF),
        in_specs=[VM] * 5,
        out_specs=VM,
        cost_estimate=pl.CostEstimate(flops=0, bytes_accessed=8 * MB, transcendentals=0),
        compiler_params=pltpu.CompilerParams(vmem_limit_bytes=8 * MB),
        name="cells",
    )(xown, ra, rb, rc, rd)


def main_kernel(
    recv, ct, wbig, gains, kern_hbm, wl, deep_out, msg,
    vup, hid_a, hid_b, act_a, act_b, act_c, cv, hs_s, ds_s, gsum, kern, pair, sem,
):
    ri = lax.axis_index("row")
    ci = col_place()
    load = pltpu.make_async_copy(kern_hbm, kern, sem.at[0])
    load.start()

    win = jnp.sum(recv[...].astype(F32), axis=0)
    m = iota((EC, 48), 0)
    q = iota((EC, 48), 1)
    j0 = jnp.where(q < 8, q, jnp.where((q == 16) | (q == 17), q - 8, -10))
    q1 = q - 24
    j1 = jnp.where((q1 >= 8) & (q1 < 16), q1 - 8, jnp.where((q1 == 18) | (q1 == 19), q1 - 10, -10))
    coef = col_weight(ext_col(m), jnp.where(q < 24, j0, j1)).astype(BF)
    lane = iota((24, 128), 1)
    for k in range(3):
        w0 = jnp.where(lane < 40, pltpu.roll(win, (128 - 40 * k) % 128, 1) if k else win, 0.0)
        w1 = pltpu.roll(win, (168 - 40 * k) % 128, 1) if k != 1 else win
        w1 = jnp.where((lane >= 40) & (lane < CIN), w1, 0.0)
        vup[k] = dotf(coef, jnp.concatenate([w0, w1], axis=0).astype(BF))

    CK = 48
    col_ok = []
    for ck in range(3):
        gc = ci * TC + ext_col(iota((CK, 1), 0) + ck * CK) - HC
        col_ok.append(jnp.where((gc >= 0) & (gc < 8 * TC), 1.0, 0.0))

    def put(act, y, ck, v):
        act[y, 1 + 3 * ck : 4 + 3 * ck] = v.reshape(3, S, W)
        if ck == 2:
            act[y, 0] = pltpu.roll(v[32:48].astype(F32), 1, 0).astype(BF)
        if ck == 0:
            act[y, L + 1] = pltpu.roll(v[:16].astype(F32), S - 1, 0).astype(BF)

    def lane_mean(v):
        half = (v[:, :128] + v[:, 128:]).astype(F32)
        return jnp.sum(half, axis=-1, keepdims=True) * (1.0 / W)

    def over_lanes(v):
        half = jnp.broadcast_to(v, (v.shape[0], 128)).astype(BF)
        return jnp.concatenate([half, half], axis=1)

    def activate(b, y, ck, before, after, act):
        gr = ri * TR + y - HR
        ok = jnp.where((gr >= 0) & (gr < 16 * TR), 1.0, 0.0)
        gain = gains[pl.ds(jnp.minimum(b, BLOCKS - 1), 1), :].astype(BF)
        keep = jnp.clip(y - 3, 0, 21)
        sl = slice(ck * CK, (ck + 1) * CK)
        h = cv[y, sl]
        if before is not None:
            h = h + before[y, sl]
        after[y, sl] = h
        s = over_lanes(lax.rsqrt(lane_mean(h * h) + 1e-06) * (col_ok[ck] * ok))
        hs = h * s
        n = hs * gain
        half = BF(0.5)
        g = half * jnp.tanh(half * n) + half
        a = n * g
        put(act, y, ck, a)
        hs_s[b, keep, sl] = hs
        ds_s[b, keep, sl] = (g + a - a * g) * (gain * s)

    def lift(g):
        ups = []
        for k in range(4):
            n = 2 * (g * 4 + k) + 5
            a = n >> 5
            t = (n & 31).astype(F32) * (1.0 / 32.0)
            ups.append(((1.0 - t) * vup[a] + t * vup[a + 1]).astype(BF))
        up = jnp.concatenate(ups, axis=0)
        own = ct[pl.ds(g * 4, 4)].reshape(4 * EC, 128)
        r = dotf(jnp.concatenate([up, own], axis=1), wbig[...])
        r = r.astype(BF)
        cv[pl.ds(g * 4, 4)] = r[:, :W].reshape(4, EC, W)
        for k in range(4):
            for ck in range(3):
                put(act_c, g * 4 + k, ck, r[k * EC + ck * CK : k * EC + (ck + 1) * CK, W:])

    def start4(g):
        for k in range(4):
            for ck in range(3):
                activate(0, g * 4 + k, ck, None, hid_a, act_a)

    def pair_kernels(i):
        i = jnp.minimum(i, 3 * BLOCKS - 1)
        b = i // 3
        q = i - 3 * b
        for c in range(0, W, 64):
            sl = slice(c, c + 64)
            k0, k1, k2 = (kern[b, p, q, sl].astype(F32) for p in range(3))
            both = 0.5 * (k0 + k2)
            mid = 0.5 * k1
            pair[b, 0, q, sl] = (both + mid).astype(BF)
            pair[b, 1, q, sl] = (both - mid).astype(BF)

    def lift_on(g, _):
        start4(g - 1)
        lift(jnp.minimum(g, ER // 4 - 1))
        pair_kernels(2 * g - 2)
        pair_kernels(2 * g - 1)
        return 0

    lift(jnp.int32(0))
    load.wait()
    lax.fori_loop(1, ER // 4 + 1, lift_on, 0)

    def conv(b, act, y0, transpose, between=()):
        between = list(between)
        dims = NT if transpose else NN

        def rows(k):
            return jnp.concatenate([act[pl.ds(y0 - 1 + k + 2 * u, 1)] for u in range(4)], axis=0)

        d0, d1, d2, d3 = rows(0), rows(1), rows(2), rows(3)
        ms = []
        for k, t in enumerate((d0 - d2, d1 + d2, d2 - d1, d1 - d3)):
            acc = None
            for q in range(3):
                dx = 2 - q if transpose else q
                if k == 1 or k == 2:
                    kk = pair[b, k - 1, q]
                else:
                    kk = kern[b, 0 if (k == 3) == transpose else 2, q]
                r = dotf(t[:, dx : dx + L].reshape(4 * EC, W), kk, dims)
                acc = r if acc is None else acc + r
                for job in between[:2]:
                    job()
                between = between[2:]
            ms.append(acc)
        e = (ms[0] + ms[1] + ms[2]).reshape(4, EC, W)
        o = (ms[1] - ms[2] - ms[3]).reshape(4, EC, W)
        for u in range(4):
            cv[y0 + 2 * u] = e[u].astype(BF)
            cv[y0 + 2 * u + 1] = o[u].astype(BF)

    def layer(b, lo, hi, act, transpose, after):
        def place(i):
            return jnp.minimum(lo + 8 * i, hi - 8)

        def rest(i):
            y0 = place(i)
            return [functools.partial(after, y0 + k, ck) for k in range(8) for ck in range(3)]

        def unit(i, _):
            conv(b, act, place(i), transpose, rest(i - 1))
            return 0

        n = (hi - lo + 7) >> 3
        conv(b, act, place(0), transpose)
        lax.fori_loop(1, n, unit, 0)
        for job in rest(n - 1):
            job()

    def forward(i, _):
        for b, src, dst in ((2 * i, (hid_a, act_a), (hid_b, act_b)), (2 * i + 1, (hid_b, act_b), (hid_a, act_a))):
            deep = b == 3
            lo = jnp.where(deep, HR, b + 1)
            hi = jnp.where(deep, HR + TR, ER - 1 - b)

            def after(y, ck, b=b, src=src, dst=dst):
                activate(b + 1, y, ck, src[0], *dst)

            layer(b, lo, hi, src[1], False, after)
        return 0

    lax.fori_loop(0, 2, forward, 0)

    save = pltpu.make_async_copy(hid_a.at[pl.ds(HR, TR)], deep_out, sem.at[1])
    save.start()

    def grad(b, y, ck, before, act):
        sl = slice(ck * CK, (ck + 1) * CK)
        u = cv[y, sl] * ds_s[b, y - 3, sl]
        hs = hs_s[b, y - 3, sl]
        old = before[y, 1 + 3 * ck : 4 + 3 * ck].reshape(CK, W)
        put(act, y, ck, old + (u - hs * over_lanes(lane_mean(u * hs))))

    def backward(i, _):
        for b, src, dst in ((3 - 2 * i, act_c, act_a), (2 - 2 * i, act_a, act_c)):

            def after(y, ck, b=b, src=src, dst=dst):
                grad(b, y, ck, src, dst)

            layer(b, HR - b, HR + TR + b, src, True, after)
        return 0

    lax.fori_loop(0, 2, backward, 0)

    e = ext_col(iota((32, EC), 1))
    qq = iota((32, EC), 0)
    j = jnp.where(qq < 10, qq, jnp.where(qq < 20, qq - 10, -10))
    own = (e >= HC) & (e < HC + TC)
    cols_t = jnp.where(own, col_weight(e, j), 0.0).astype(BF)
    gsum[...] = jnp.zeros_like(gsum)

    def gather(g, _):
        for k in range(4):
            y = 4 * g + k + HR
            t = dotf(cols_t, act_c[y, 1 : 1 + L].reshape(EC, W))
            n = 2 * y + 5
            a = n >> 5
            w = (n & 31).astype(F32) * (1.0 / 32.0)
            gsum[a] = gsum[a] + (1.0 - w) * t
            gsum[a + 1] = gsum[a + 1] + w * t
        return 0

    lax.fori_loop(0, TR // 4, gather, 0)
    g = jnp.concatenate([gsum[0], gsum[1], gsum[2]], axis=1)
    g_hi = g.astype(BF)
    g_lo = (g - g_hi.astype(F32)).astype(BF)
    o = dotf(g_hi, wl[...]) + dotf(g_lo, wl[...])
    o = jnp.where(iota((32, 128), 0) < 10, o[:, :128], o[:, 128:]).astype(BF)[:24]

    def spread(d, _):
        for k in range(8):
            msg[8 * d + k] = o
        return 0

    lax.fori_loop(0, 16, spread, 0)
    save.wait()


def main(recv, ct, wbig, gains, kern, wl):
    return pl.pallas_call(
        main_kernel,
        out_shape=[
            jax.ShapeDtypeStruct((TR, EC, W), BF),
            jax.ShapeDtypeStruct((128, 24, 128), BF),
        ],
        in_specs=[VM] * 4 + [pl.BlockSpec(memory_space=pl.ANY), VM],
        out_specs=[pl.BlockSpec(memory_space=pltpu.HBM), VM],
        scratch_shapes=[
            pltpu.VMEM((3, EC, 128), F32),
            pltpu.VMEM((ER, EC, W), BF),
            pltpu.VMEM((ER, EC, W), BF),
            pltpu.VMEM((ER, L + 2, S, W), BF),
            pltpu.VMEM((ER, L + 2, S, W), BF),
            pltpu.VMEM((ER, L + 2, S, W), BF),
            pltpu.VMEM((ER, EC, W), BF),
            pltpu.VMEM((BLOCKS + 1, ER - 6, EC, W), BF),
            pltpu.VMEM((BLOCKS + 1, ER - 6, EC, W), BF),
            pltpu.VMEM((3, 32, W), F32),
            pltpu.VMEM((BLOCKS, 3, 3, W, W), BF),
            pltpu.VMEM((BLOCKS, 2, 3, W, W), BF),
            pltpu.SemaphoreType.DMA((2,)),
        ],
        compiler_params=pltpu.CompilerParams(vmem_limit_bytes=48 * MB),
        name="main",
    )(recv, ct, wbig, gains, kern, wl)


def head_kernel(hid, wht, after, fine, mixed):
    perm = one_hot(ext_col(iota((EC, TC), 0)) - HC == iota((EC, TC), 1))
    for y in range(TR):
        mixed[y] = dotf(wht[...], hid[y], NT).astype(BF)
    out = dotf(mixed[...].reshape(TR * 80, EC), perm).astype(BF).reshape(TR, 80, TC)
    fine[...] = out[:, :CIN]


def head(hid, wht, after):
    return pl.pallas_call(
        head_kernel,
        out_shape=jax.ShapeDtypeStruct((TR, CIN, TC), BF),
        in_specs=[VM, VM, pl.BlockSpec(memory_space=pl.ANY)],
        out_specs=VM,
        scratch_shapes=[pltpu.VMEM((TR, 80, EC), BF)],
        cost_estimate=pl.CostEstimate(flops=0, bytes_accessed=6 * MB, transcendentals=0),
        compiler_params=pltpu.CompilerParams(vmem_limit_bytes=8 * MB),
        name="head",
    )(hid, wht, after)


def blank_kernel(after, out):
    out[...] = jnp.zeros_like(out)


def blank(after):
    return pl.pallas_call(
        blank_kernel,
        out_shape=jax.ShapeDtypeStruct((LAT_DEV, CIN, LON_DEV), F32),
        grid=(5,),
        in_specs=[pl.BlockSpec(memory_space=pl.ANY)],
        out_specs=pl.BlockSpec((9, CIN, LON_DEV), lambda i: (i, 0, 0)),
        cost_estimate=pl.CostEstimate(flops=0, bytes_accessed=4 * MB, transcendentals=0),
        compiler_params=pltpu.CompilerParams(vmem_limit_bytes=8 * MB),
        name="blank",
    )(after)


def place_kernel(ro, co, recv, zero, out, acc, sem):
    first_row = ro[0] - 1 - LAT_DEV * lax.axis_index("row")
    off = co[0] - 1 - LON_DEV * col_place()
    q = iota((192, 512), 0)
    lane = iota((192, 512), 1)
    h = lane >> 8
    lj = lane & 255
    c = q // 24
    j = q - c * 24 - 10 * h
    sel = one_hot((j >= 0) & (j < 10) & (lj == off + 8 * c + j) & (lj < LON_DEV))
    acc[...] = jnp.zeros_like(acc)

    def rows(g, _):
        for u in range(4):
            r = 4 * g + u
            a = recv[:, r].astype(F32).reshape(192, 128).astype(BF)
            o = dotf(a, sel, TN)
            for k in range(3):
                acc[r + k, :40] = acc[r + k, :40] + o[40 * k : 40 * k + 40, :LON_DEV]
                acc[r + k, 40:] = acc[r + k, 40:] + o[40 * k : 40 * k + 38, 256 : 256 + LON_DEV]
        return 0

    lax.fori_loop(0, 4, rows, 0)
    lo = jnp.clip(-first_row, 0, 18)
    hi = jnp.clip(LAT_DEV - first_row, lo, 18)

    def copy(i):
        li = jnp.clip(first_row + i, 0, LAT_DEV - 1)
        return pltpu.make_async_copy(acc.at[i], out.at[li], sem)

    def start(i, _):
        copy(i).start()
        return 0

    def wait(i, _):
        copy(i).wait()
        return 0

    lax.fori_loop(lo, hi, start, 0)
    lax.fori_loop(lo, hi, wait, 0)


def place(ro, co, recv, zero):
    hbm = pl.BlockSpec(memory_space=pltpu.HBM)
    return pl.pallas_call(
        place_kernel,
        out_shape=jax.ShapeDtypeStruct((LAT_DEV, CIN, LON_DEV), F32),
        in_specs=[SM, SM, VM, hbm],
        out_specs=hbm,
        input_output_aliases={3: 0},
        scratch_shapes=[pltpu.VMEM((18, CIN, LON_DEV), F32), pltpu.SemaphoreType.DMA(())],
        compiler_params=pltpu.CompilerParams(vmem_limit_bytes=16 * MB),
        name="place",
    )(ro, co, recv, zero)


def shards(coarse, ro, co, static, w_lift, w_static, gains, kern, w_head, cot):
    xown, pa, pb = own_rows(static, cot)
    near = [(i, i ^ 1) for i in range(16)]
    far = [(i, j) for i in range(16) for j in [i + 1 if i & 1 else i - 1] if 0 <= j < 16]
    ra = lax.ppermute(pa, "row", near)
    rb = lax.ppermute(pb, "row", far)
    send = pack(ro, co, coarse, pa)
    pc, pd = edges(xown, ra, rb)
    near = [(i, i ^ 1) for i in range(8)]
    far = [(i, j) for i in range(8) for j in [i + 1 if i & 1 else i - 1] if 0 <= j < 8]
    send, pc, pd = lax.optimization_barrier((send, pc, pd))
    rc = lax.ppermute(pc, ("sec", "col"), near)
    rd = lax.ppermute(pd, ("sec", "col"), far)
    recv = lax.all_to_all(send, ("sec", "row", "col"), 0, 0, tiled=True)
    ct = cells(xown, ra, rb, rc, rd)

    wht = w_head.T
    zero = jnp.zeros
    wbig = jnp.concatenate(
        [
            jnp.concatenate([w_lift, zero((50, W), BF), zero((80, W), BF), w_static, zero((44, W), BF)], 0),
            jnp.concatenate([zero((128, W), BF), wht, zero((50, W), BF)], 0),
        ],
        1,
    )
    wht80 = jnp.concatenate([wht, zero((2, W), BF)], 0)
    wl = jnp.concatenate([w_lift, zero((2, W), BF)], 0).reshape(2, 40, W).transpose(2, 0, 1)
    wl = jnp.concatenate(
        [jnp.pad(wl, ((0, 0), (0, 0), (40 * k, 88 - 40 * k))).reshape(W, 256) for k in range(3)], 0
    )
    deep, msg = main(recv, ct, wbig, gains, kern, wl)
    back = lax.all_to_all(msg, ("sec", "row", "col"), 0, 0, tiled=True)
    return head(deep, wht80, msg), place(ro, co, back.reshape(2, 16, 4, 24, 128), blank(msg))


def solution(mesh):
    tile = P("row", None, ("sec", "col"))
    in_specs = (tile, P(), P(), tile, P(), P(), P(), P(), P(), tile)
    return jax.shard_map(shards, mesh=mesh, in_specs=in_specs, out_specs=(tile, tile), check_vma=False)
```

```python
import functools

import jax
import jax.numpy as jnp
from jax import lax
from jax.experimental import pallas as pl
from jax.experimental.pallas import tpu as pltpu
from jax.sharding import PartitionSpec as P

R = 16
CIN = 78
W = 256
BLOCKS = 4
TR = 16
TC = 128
LAT_DEV = 45
LON_DEV = 180
HR = 6
HC = 8
ER = TR + 2 * HR
L = 9
S = 16
EC = L * S
BF = jnp.bfloat16
F32 = jnp.float32
VM = pl.BlockSpec(memory_space=pltpu.VMEM)
SM = pl.BlockSpec(memory_space=pltpu.SMEM)
MB = 2**20
NT = (((1,), (1,)), ((), ()))
NN = (((1,), (0,)), ((), ()))
TN = (((0,), (0,)), ((), ()))


def dotf(a, b, dims=NN):
    return lax.dot_general(a, b, dims, preferred_element_type=F32)


def iota(shape, dim):
    return lax.broadcasted_iota(jnp.int32, shape, dim)


def ext_col(m):
    return (m & 15) * L + (m >> 4)


def one_hot(cond):
    return jnp.where(cond, 1.0, 0.0).astype(BF)


def col_weight(e, j):
    n = 2 * e + 1
    a = n >> 5
    t = (n & 31).astype(F32) * (1.0 / 32.0)
    return jnp.where(j == a, 1.0 - t, 0.0) + jnp.where(j == a + 1, t, 0.0)


def col_place():
    return lax.axis_index("sec") * 4 + lax.axis_index("col")


def rows_kernel(static, cot, xown, pa, pb):
    xown[...] = jnp.zeros_like(xown)
    xown[:, :CIN, :] = cot[...]
    xown[:, 80:84, :] = static[...]
    odd = (lax.axis_index("row") & 1) == 1
    pa[...] = xown[pl.ds(jnp.where(odd, 0, TR - HR), HR)]
    pb[...] = xown[pl.ds(jnp.where(odd, TR - HR, 0), HR)]


def own_rows(static, cot):
    return pl.pallas_call(
        rows_kernel,
        out_shape=[
            jax.ShapeDtypeStruct((TR, 128, 128), BF),
            jax.ShapeDtypeStruct((HR, 128, 128), BF),
            jax.ShapeDtypeStruct((HR, 128, 128), BF),
        ],
        in_specs=[VM] * 2,
        out_specs=[VM] * 3,
        cost_estimate=pl.CostEstimate(flops=0, bytes_accessed=2 * MB, transcendentals=0),
        compiler_params=pltpu.CompilerParams(vmem_limit_bytes=8 * MB),
        name="own_rows",
    )(static, cot)


def pack_kernel(ro, co, coarse, after, send, xs, prod, sem):
    ri = lax.axis_index("row")
    ci = col_place()
    first_row = ro[0] - 1 - LAT_DEV * ri
    off = co[0] - 1 - LON_DEV * ci
    start = jnp.clip(first_row, 0, LAT_DEV - 18)
    copy = pltpu.make_async_copy(coarse.at[pl.ds(start, 18)], xs, sem)
    copy.start()
    lj = iota((144, LON_DEV), 1)
    q = iota((144, LON_DEV), 0)
    tail = q - 80
    j_tail = jnp.where((tail & 7) < 6, 8 * (tail >> 3) + 8 + (tail & 1), -100000)
    j = jnp.where(q < 80, jnp.where(q < 66, q, -100000), j_tail)
    sel = one_hot(lj == off + j)
    prod[:, :, CIN:] = jnp.zeros((18, 144, 128 - CIN), F32)
    copy.wait()

    def rows(g, _):
        for k in range(6):
            i = 6 * g + k
            li = first_row + i
            ok = jnp.where((li >= 0) & (li < LAT_DEV), 1.0, 0.0)
            prod[i, :, :CIN] = dotf(sel, xs[jnp.clip(li - start, 0, 17)], NT) * ok
        return 0

    lax.fori_loop(0, 3, rows, 0)
    part = iota((144, 128), 1) >> 5
    low = iota((64, 128), 0) & 7

    def dest(r):
        ms = []
        for h in range(3):
            m = None
            for k in range(4):
                p = prod[2 * r + k]
                p = p if k == h else pltpu.roll(p, 32 * (k - h) % 128, 1)
                m = p if m is None else jnp.where(part == k, p, m)
            ms.append(m)
        tails = jnp.where(low < 2, ms[0][80:], jnp.where(low < 4, ms[1][80:], ms[2][80:]))
        for cc in range(8):
            d = (cc // 4) * 32 + r * 4 + cc % 4
            sl = slice(8 * cc, 8 * cc + 8)
            send[d] = jnp.concatenate([m[sl] for m in ms] + [tails[sl]], axis=0).astype(BF)

    def dests(g, _):
        for k in range(2):
            dest(2 * g + k)
        return 0

    lax.fori_loop(0, 4, dests, 0)


def pack(ro, co, coarse, after):
    return pl.pallas_call(
        pack_kernel,
        out_shape=jax.ShapeDtypeStruct((64, 32, 128), BF),
        in_specs=[SM, SM, pl.BlockSpec(memory_space=pltpu.HBM), pl.BlockSpec(memory_space=pl.ANY)],
        out_specs=VM,
        scratch_shapes=[
            pltpu.VMEM((18, CIN, LON_DEV), BF),
            pltpu.VMEM((18, 144, 128), F32),
            pltpu.SemaphoreType.DMA(()),
        ],
        cost_estimate=pl.CostEstimate(flops=0, bytes_accessed=8 * MB, transcendentals=0),
        compiler_params=pltpu.CompilerParams(vmem_limit_bytes=57 * MB),
        name="pack",
    )(ro, co, coarse, after)


def edge_kernel(xown, ra, rb, pc, pd, edge):
    odd = (lax.axis_index("row") & 1) == 1
    oddc = (col_place() & 1) == 1
    q = iota((16, 128), 0)
    sel = one_hot(iota((16, 128), 1) == jnp.where(q < 8, q, q + 112))

    def do(y0, x):
        n = x.shape[0]
        r = dotf(sel, x.reshape(n * 128, 128), NT)
        for k in range(n):
            edge[y0 + k] = r[:, k * 128 : (k + 1) * 128]

    do(HR, xown[...])
    a = ra[...]
    b = rb[...]
    do(0, jnp.where(odd, a, b))
    do(HR + TR, jnp.where(odd, b, a))
    left = edge[:, :8, :].reshape(ER * 8, 128)
    right = edge[:, 8:, :].reshape(ER * 8, 128)
    pc[...] = jnp.where(oddc, left, right).astype(BF)
    pd[...] = jnp.where(oddc, right, left).astype(BF)


def edges(xown, ra, rb):
    return pl.pallas_call(
        edge_kernel,
        out_shape=[
            jax.ShapeDtypeStruct((ER * 8, 128), BF),
            jax.ShapeDtypeStruct((ER * 8, 128), BF),
        ],
        in_specs=[VM] * 3,
        out_specs=[VM] * 2,
        scratch_shapes=[pltpu.VMEM((ER, 16, 128), F32)],
        cost_estimate=pl.CostEstimate(flops=0, bytes_accessed=4 * MB, transcendentals=0),
        compiler_params=pltpu.CompilerParams(vmem_limit_bytes=8 * MB),
        name="edges",
    )(xown, ra, rb)


def cells_kernel(xown, ra, rb, rc, rd, ct):
    odd = (lax.axis_index("row") & 1) == 1
    oddc = (col_place() & 1) == 1
    perm = one_hot(ext_col(iota((EC, 128), 0)) - HC == iota((EC, 128), 1))
    m = iota((2 * EC, 16), 0)
    q = iota((2 * EC, 16), 1)
    y2 = (m >= EC).astype(jnp.int32)
    e2 = ext_col(m - y2 * EC)
    same = y2 == (q >> 3)
    perm_l = one_hot(same & (e2 == (q & 7)))
    perm_r = one_hot(same & (e2 - (HC + TC) == (q & 7)))

    def do(y, x):
        rows = pl.ds(pl.multiple_of(y * 8, 16), 16)
        c = rc[rows, :]
        d = rd[rows, :]
        halo = dotf(perm_l, jnp.where(oddc, c, d)) + dotf(perm_r, jnp.where(oddc, d, c))
        for k in range(2):
            ct[y + k] = (dotf(perm, x[k], NT) + halo[k * EC : (k + 1) * EC]).astype(BF)

    def mid(i, _):
        for k in range(2):
            y = 4 * i + 2 * k
            do(y + HR, xown[pl.ds(y, 2)])
        return 0

    lax.fori_loop(0, TR // 4, mid, 0)
    for y in range(0, HR, 2):
        a = ra[y : y + 2]
        b = rb[y : y + 2]
        do(y, jnp.where(odd, a, b))
        do(y + HR + TR, jnp.where(odd, b, a))


def cells(xown, ra, rb, rc, rd):
    return pl.pallas_call(
        cells_kernel,
        out_shape=jax.ShapeDtypeStruct((ER, EC, 128), BF),
        in_specs=[VM] * 5,
        out_specs=VM,
        cost_estimate=pl.CostEstimate(flops=0, bytes_accessed=8 * MB, transcendentals=0),
        compiler_params=pltpu.CompilerParams(vmem_limit_bytes=8 * MB),
        name="cells",
    )(xown, ra, rb, rc, rd)


def fold_kernel(recv, out):
    out[...] = jnp.sum(recv[...].astype(F32), axis=0).astype(BF)


def fold(recv):
    return pl.pallas_call(
        fold_kernel,
        out_shape=jax.ShapeDtypeStruct((32, 128), BF),
        in_specs=[VM],
        out_specs=VM,
        compiler_params=pltpu.CompilerParams(vmem_limit_bytes=4 * MB),
        name="fold",
    )(recv)


def spread_kernel(mine, other, out):
    o = (mine[...] + other[...]).astype(BF)
    for d in range(64):
        out[d] = o


def spread(mine, other):
    return pl.pallas_call(
        spread_kernel,
        out_shape=jax.ShapeDtypeStruct((64, 32, 128), BF),
        in_specs=[VM] * 2,
        out_specs=VM,
        compiler_params=pltpu.CompilerParams(vmem_limit_bytes=4 * MB),
        name="spread",
    )(mine, other)


def main_kernel(
    win_a, win_b, ct, wbig, gains, kern_hbm, wl, deep_out, msg,
    vup, hid_a, hid_b, act_a, act_b, act_c, cv, hs_s, ds_s, gsum, kern, pair, sem,
):
    ri = lax.axis_index("row")
    ci = col_place()
    load = pltpu.make_async_copy(kern_hbm, kern, sem.at[0])
    load.start()

    win = win_a[...].astype(F32) + win_b[...].astype(F32)
    odd = (ri & 1) == 1
    win = jnp.where(odd, pltpu.roll(win, 96, 1), win)
    m = iota((EC, 96), 0)
    q = iota((EC, 96), 1)
    h = q >> 5
    q = q & 31
    j = jnp.where((q >> 3) == h, q & 7, jnp.where((q >> 1) == 12 + h, 8 + (q & 1), -10))
    coef = col_weight(ext_col(m), j).astype(BF)
    lane = iota((32, 128), 1)
    for k in range(3):
        parts = []
        for h in range(3):
            w = win if h == k else pltpu.roll(win, 32 * (h - k) % 128, 1)
            parts.append(jnp.where(((lane >> 5) == h) & (lane < CIN), w, 0.0))
        vup[k] = dotf(coef, jnp.concatenate(parts, axis=0).astype(BF))

    CK = 48
    col_ok = []
    for ck in range(3):
        gc = ci * TC + ext_col(iota((CK, 1), 0) + ck * CK) - HC
        col_ok.append(jnp.where((gc >= 0) & (gc < 8 * TC), 1.0, 0.0))

    def put(act, y, ck, v):
        act[y, 1 + 3 * ck : 4 + 3 * ck] = v.reshape(3, S, W)
        if ck == 2:
            act[y, 0] = pltpu.roll(v[32:48].astype(F32), 1, 0).astype(BF)
        if ck == 0:
            act[y, L + 1] = pltpu.roll(v[:16].astype(F32), S - 1, 0).astype(BF)

    def lane_mean(v):
        half = (v[:, :128] + v[:, 128:]).astype(F32)
        return jnp.sum(half, axis=-1, keepdims=True) * (1.0 / W)

    def over_lanes(v):
        half = jnp.broadcast_to(v, (v.shape[0], 128)).astype(BF)
        return jnp.concatenate([half, half], axis=1)

    def activate(b, y, ck, before, after, act):
        gr = ri * TR + y - HR
        ok = jnp.where((gr >= 0) & (gr < 16 * TR), 1.0, 0.0)
        gain = gains[pl.ds(jnp.minimum(b, BLOCKS - 1), 1), :].astype(BF)
        keep = jnp.clip(y - 3, 0, 21)
        sl = slice(ck * CK, (ck + 1) * CK)
        h = cv[y, sl]
        if before is not None:
            h = h + before[y, sl]
        after[y, sl] = h
        s = over_lanes(lax.rsqrt(lane_mean(h * h) + 1e-06) * (col_ok[ck] * ok))
        hs = h * s
        n = hs * gain
        half = BF(0.5)
        g = half * jnp.tanh(half * n) + half
        a = n * g
        put(act, y, ck, a)
        hs_s[b, keep, sl] = hs
        ds_s[b, keep, sl] = (g + a - a * g) * (gain * s)

    def lift(g):
        ups = []
        for k in range(4):
            n = 2 * (g * 4 + k) + 5
            a = n >> 5
            t = (n & 31).astype(F32) * (1.0 / 32.0)
            ups.append(((1.0 - t) * vup[a] + t * vup[a + 1]).astype(BF))
        up = jnp.concatenate(ups, axis=0)
        own = ct[pl.ds(g * 4, 4)].reshape(4 * EC, 128)
        r = dotf(jnp.concatenate([up, own], axis=1), wbig[...])
        r = r.astype(BF)
        cv[pl.ds(g * 4, 4)] = r[:, :W].reshape(4, EC, W)
        for k in range(4):
            for ck in range(3):
                put(act_c, g * 4 + k, ck, r[k * EC + ck * CK : k * EC + (ck + 1) * CK, W:])

    def start4(g):
        for k in range(4):
            for ck in range(3):
                activate(0, g * 4 + k, ck, None, hid_a, act_a)

    def pair_kernels(i):
        i = jnp.minimum(i, 3 * BLOCKS - 1)
        b = i // 3
        q = i - 3 * b
        for c in range(0, W, 64):
            sl = slice(c, c + 64)
            k0, k1, k2 = (kern[b, p, q, sl].astype(F32) for p in range(3))
            both = 0.5 * (k0 + k2)
            mid = 0.5 * k1
            pair[b, 0, q, sl] = (both + mid).astype(BF)
            pair[b, 1, q, sl] = (both - mid).astype(BF)

    def lift_on(g, _):
        start4(g - 1)
        lift(jnp.minimum(g, ER // 4 - 1))
        pair_kernels(2 * g - 2)
        pair_kernels(2 * g - 1)
        return 0

    lift(jnp.int32(0))
    load.wait()
    lax.fori_loop(1, ER // 4 + 1, lift_on, 0)

    def conv(b, act, y0, transpose, between=()):
        between = list(between)
        dims = NT if transpose else NN

        def rows(k):
            return jnp.concatenate([act[pl.ds(y0 - 1 + k + 2 * u, 1)] for u in range(4)], axis=0)

        d0, d1, d2, d3 = rows(0), rows(1), rows(2), rows(3)
        ms = []
        for k, t in enumerate((d0 - d2, d1 + d2, d2 - d1, d1 - d3)):
            acc = None
            for q in range(3):
                dx = 2 - q if transpose else q
                if k == 1 or k == 2:
                    kk = pair[b, k - 1, q]
                else:
                    kk = kern[b, 0 if (k == 3) == transpose else 2, q]
                r = dotf(t[:, dx : dx + L].reshape(4 * EC, W), kk, dims)
                acc = r if acc is None else acc + r
                for job in between[:2]:
                    job()
                between = between[2:]
            ms.append(acc)
        e = (ms[0] + ms[1] + ms[2]).reshape(4, EC, W)
        o = (ms[1] - ms[2] - ms[3]).reshape(4, EC, W)
        for u in range(4):
            cv[y0 + 2 * u] = e[u].astype(BF)
            cv[y0 + 2 * u + 1] = o[u].astype(BF)

    def layer(b, lo, hi, act, transpose, after):
        def place(i):
            return jnp.minimum(lo + 8 * i, hi - 8)

        def rest(i):
            y0 = place(i)
            return [functools.partial(after, y0 + k, ck) for k in range(8) for ck in range(3)]

        def unit(i, _):
            conv(b, act, place(i), transpose, rest(i - 1))
            return 0

        n = (hi - lo + 7) >> 3
        conv(b, act, place(0), transpose)
        lax.fori_loop(1, n, unit, 0)
        for job in rest(n - 1):
            job()

    def forward(i, _):
        for b, src, dst in ((2 * i, (hid_a, act_a), (hid_b, act_b)), (2 * i + 1, (hid_b, act_b), (hid_a, act_a))):
            deep = b == 3
            lo = jnp.where(deep, HR, b + 1)
            hi = jnp.where(deep, HR + TR, ER - 1 - b)

            def after(y, ck, b=b, src=src, dst=dst):
                activate(b + 1, y, ck, src[0], *dst)

            layer(b, lo, hi, src[1], False, after)
        return 0

    lax.fori_loop(0, 2, forward, 0)

    save = pltpu.make_async_copy(hid_a.at[pl.ds(HR, TR)], deep_out, sem.at[1])
    save.start()

    def grad(b, y, ck, before, act):
        sl = slice(ck * CK, (ck + 1) * CK)
        u = cv[y, sl] * ds_s[b, y - 3, sl]
        hs = hs_s[b, y - 3, sl]
        old = before[y, 1 + 3 * ck : 4 + 3 * ck].reshape(CK, W)
        put(act, y, ck, old + (u - hs * over_lanes(lane_mean(u * hs))))

    def backward(i, _):
        for b, src, dst in ((3 - 2 * i, act_c, act_a), (2 - 2 * i, act_a, act_c)):

            def after(y, ck, b=b, src=src, dst=dst):
                grad(b, y, ck, src, dst)

            layer(b, HR - b, HR + TR + b, src, True, after)
        return 0

    lax.fori_loop(0, 2, backward, 0)

    e = ext_col(iota((32, EC), 1))
    qq = iota((32, EC), 0)
    j = jnp.where(qq < 10, qq, jnp.where(qq < 20, qq - 10, jnp.where(qq < 30, qq - 20, -10)))
    own = (e >= HC) & (e < HC + TC)
    cols_t = jnp.where(own, col_weight(e, j), 0.0).astype(BF)
    gsum[...] = jnp.zeros_like(gsum)

    def gather(g, _):
        for k in range(4):
            y = 4 * g + k + HR
            t = dotf(cols_t, act_c[y, 1 : 1 + L].reshape(EC, W))
            n = 2 * y + 5
            a = n >> 5
            w = (n & 31).astype(F32) * (1.0 / 32.0)
            gsum[a] = gsum[a] + (1.0 - w) * t
            gsum[a + 1] = gsum[a + 1] + w * t
        return 0

    lax.fori_loop(0, TR // 4, gather, 0)
    g = jnp.concatenate([gsum[0], gsum[1], gsum[2]], axis=1)
    g_hi = g.astype(BF)
    g_lo = (g - g_hi.astype(F32)).astype(BF)
    o = dotf(g_hi, wl[...]) + dotf(g_lo, wl[...])
    row = iota((32, 128), 0)
    o = jnp.where(row < 10, o[:, :128], jnp.where(row < 20, o[:, 128:256], o[:, 256:]))
    msg[...] = jnp.where(odd, pltpu.roll(o, 32, 1), o)
    save.wait()


def main(win_a, win_b, ct, wbig, gains, kern, wl):
    return pl.pallas_call(
        main_kernel,
        out_shape=[
            jax.ShapeDtypeStruct((TR, EC, W), BF),
            jax.ShapeDtypeStruct((32, 128), F32),
        ],
        in_specs=[VM] * 5 + [pl.BlockSpec(memory_space=pl.ANY), VM],
        out_specs=[pl.BlockSpec(memory_space=pltpu.HBM), VM],
        scratch_shapes=[
            pltpu.VMEM((3, EC, 128), F32),
            pltpu.VMEM((ER, EC, W), BF),
            pltpu.VMEM((ER, EC, W), BF),
            pltpu.VMEM((ER, L + 2, S, W), BF),
            pltpu.VMEM((ER, L + 2, S, W), BF),
            pltpu.VMEM((ER, L + 2, S, W), BF),
            pltpu.VMEM((ER, EC, W), BF),
            pltpu.VMEM((BLOCKS + 1, ER - 6, EC, W), BF),
            pltpu.VMEM((BLOCKS + 1, ER - 6, EC, W), BF),
            pltpu.VMEM((3, 32, W), F32),
            pltpu.VMEM((BLOCKS, 3, 3, W, W), BF),
            pltpu.VMEM((BLOCKS, 2, 3, W, W), BF),
            pltpu.SemaphoreType.DMA((2,)),
        ],
        compiler_params=pltpu.CompilerParams(vmem_limit_bytes=50 * MB),
        name="main",
    )(win_a, win_b, ct, wbig, gains, kern, wl)


def head_kernel(hid, wht, after, fine, mixed):
    perm = one_hot(ext_col(iota((EC, TC), 0)) - HC == iota((EC, TC), 1))
    for y in range(TR):
        mixed[y] = dotf(wht[...], hid[y], NT).astype(BF)
    out = dotf(mixed[...].reshape(TR * 80, EC), perm).astype(BF).reshape(TR, 80, TC)
    fine[...] = out[:, :CIN]


def head(hid, wht, after):
    return pl.pallas_call(
        head_kernel,
        out_shape=jax.ShapeDtypeStruct((TR, CIN, TC), BF),
        in_specs=[VM, VM, pl.BlockSpec(memory_space=pl.ANY)],
        out_specs=VM,
        scratch_shapes=[pltpu.VMEM((TR, 80, EC), BF)],
        cost_estimate=pl.CostEstimate(flops=0, bytes_accessed=6 * MB, transcendentals=0),
        compiler_params=pltpu.CompilerParams(vmem_limit_bytes=8 * MB),
        name="head",
    )(hid, wht, after)


def blank_kernel(after, out):
    out[...] = jnp.zeros_like(out)


def blank(after):
    return pl.pallas_call(
        blank_kernel,
        out_shape=jax.ShapeDtypeStruct((LAT_DEV, CIN, LON_DEV), F32),
        grid=(5,),
        in_specs=[pl.BlockSpec(memory_space=pl.ANY)],
        out_specs=pl.BlockSpec((9, CIN, LON_DEV), lambda i: (i, 0, 0)),
        cost_estimate=pl.CostEstimate(flops=0, bytes_accessed=4 * MB, transcendentals=0),
        compiler_params=pltpu.CompilerParams(vmem_limit_bytes=8 * MB),
        name="blank",
    )(after)


def place_kernel(ro, co, recv, zero, out, acc, sem):
    first_row = ro[0] - 1 - LAT_DEV * lax.axis_index("row")
    off = co[0] - 1 - LON_DEV * col_place()
    q = iota((256, 768), 0)
    lane = iota((256, 768), 1)
    lj = lane & 255
    j = (q & 31) - 10 * (lane >> 8)
    sel = one_hot((j >= 0) & (j < 10) & (lj == off + 8 * (q >> 5) + j) & (lj < LON_DEV))
    acc[...] = jnp.zeros_like(acc)

    def rows(g, _):
        for u in range(4):
            r = 4 * g + u
            o = dotf(recv[:, r].reshape(256, 128), sel, TN)
            for k in range(4):
                for h in range(3):
                    n = min(32, CIN - 32 * h)
                    sl = slice(32 * h, 32 * h + n)
                    part = o[32 * k : 32 * k + n, 256 * h : 256 * h + LON_DEV]
                    acc[2 * r + k, sl] = acc[2 * r + k, sl] + part
        return 0

    lax.fori_loop(0, 2, rows, 0)
    lo = jnp.clip(-first_row, 0, 18)
    hi = jnp.clip(LAT_DEV - first_row, lo, 18)

    def copy(i):
        li = jnp.clip(first_row + i, 0, LAT_DEV - 1)
        return pltpu.make_async_copy(acc.at[i], out.at[li], sem)

    def start(i, _):
        copy(i).start()
        return 0

    def wait(i, _):
        copy(i).wait()
        return 0

    lax.fori_loop(lo, hi, start, 0)
    lax.fori_loop(lo, hi, wait, 0)


def place(ro, co, recv, zero):
    hbm = pl.BlockSpec(memory_space=pltpu.HBM)
    return pl.pallas_call(
        place_kernel,
        out_shape=jax.ShapeDtypeStruct((LAT_DEV, CIN, LON_DEV), F32),
        in_specs=[SM, SM, VM, hbm],
        out_specs=hbm,
        input_output_aliases={3: 0},
        scratch_shapes=[pltpu.VMEM((18, CIN, LON_DEV), F32), pltpu.SemaphoreType.DMA(())],
        compiler_params=pltpu.CompilerParams(vmem_limit_bytes=16 * MB),
        name="place",
    )(ro, co, recv, zero)


def shards(coarse, ro, co, static, w_lift, w_static, gains, kern, w_head, cot):
    xown, pa, pb = own_rows(static, cot)
    near = [(i, i ^ 1) for i in range(16)]
    far = [(i, j) for i in range(16) for j in [i + 1 if i & 1 else i - 1] if 0 <= j < 16]
    ra = lax.ppermute(pa, "row", near)
    rb = lax.ppermute(pb, "row", far)
    send = pack(ro, co, coarse, pa)
    pc, pd = edges(xown, ra, rb)
    near = [(i, i ^ 1) for i in range(8)]
    far = [(i, j) for i in range(8) for j in [i + 1 if i & 1 else i - 1] if 0 <= j < 8]
    send, pc, pd = lax.optimization_barrier((send, pc, pd))
    rc = lax.ppermute(pc, ("sec", "col"), near)
    rd = lax.ppermute(pd, ("sec", "col"), far)
    groups = [
        [sec * 64 + row * 4 + col for sec in range(2) for row in range(core, 16, 2) for col in range(4)]
        for core in range(2)
    ]

    def swap(x):
        return lax.all_to_all(x, ("sec", "row", "col"), 0, 0, axis_index_groups=groups, tiled=True)

    mates = [(i, i ^ 1) for i in range(16)]
    win_a = fold(swap(send))
    win_b = lax.ppermute(win_a, "row", mates)
    ct = cells(xown, ra, rb, rc, rd)

    wht = w_head.T
    zero = jnp.zeros
    wbig = jnp.concatenate(
        [
            jnp.concatenate([w_lift, zero((50, W), BF), zero((80, W), BF), w_static, zero((44, W), BF)], 0),
            jnp.concatenate([zero((128, W), BF), wht, zero((50, W), BF)], 0),
        ],
        1,
    )
    wht80 = jnp.concatenate([wht, zero((2, W), BF)], 0)
    wl = jnp.concatenate([w_lift, zero((18, W), BF)], 0).reshape(3, 32, W).transpose(2, 0, 1)
    wl = jnp.concatenate(
        [jnp.pad(wl, ((0, 0), (0, 0), (32 * k, 96 - 32 * k))).reshape(W, 384) for k in range(3)], 0
    )
    deep, own = main(win_a, win_b, ct, wbig, gains, kern, wl)
    msg = spread(own, lax.ppermute(own, "row", mates))
    back = swap(msg)
    return head(deep, wht80, msg), place(ro, co, back.reshape(2, 8, 4, 32, 128), blank(msg))


def solution(mesh):
    tile = P("row", None, ("sec", "col"))
    in_specs = (tile, P(), P(), tile, P(), P(), P(), P(), P(), tile)
    return jax.shard_map(shards, mesh=mesh, in_specs=in_specs, out_specs=(tile, tile), check_vma=False)
```

```python
import functools

import jax
import jax.numpy as jnp
from jax import lax
from jax.experimental import pallas as pl
from jax.experimental.pallas import tpu as pltpu
from jax.sharding import PartitionSpec as P

R = 16
CIN = 78
W = 256
BLOCKS = 4
TR = 16
TC = 128
LAT_DEV = 45
LON_DEV = 180
HR = 6
HC = 8
ER = TR + 2 * HR
L = 9
S = 16
EC = L * S
BF = jnp.bfloat16
F32 = jnp.float32
VM = pl.BlockSpec(memory_space=pltpu.VMEM)
SM = pl.BlockSpec(memory_space=pltpu.SMEM)
MB = 2**20
NT = (((1,), (1,)), ((), ()))
NN = (((1,), (0,)), ((), ()))
TN = (((0,), (0,)), ((), ()))


def dotf(a, b, dims=NN):
    return lax.dot_general(a, b, dims, preferred_element_type=F32)


def iota(shape, dim):
    return lax.broadcasted_iota(jnp.int32, shape, dim)


def ext_col(m):
    return (m & 15) * L + (m >> 4)


def one_hot(cond):
    return jnp.where(cond, 1.0, 0.0).astype(BF)


def col_weight(e, j):
    n = 2 * e + 1
    a = n >> 5
    t = (n & 31).astype(F32) * (1.0 / 32.0)
    return jnp.where(j == a, 1.0 - t, 0.0) + jnp.where(j == a + 1, t, 0.0)


def col_place():
    return lax.axis_index("sec") * 4 + lax.axis_index("col")


def rows_kernel(static, cot, xown, pa, pb):
    xown[...] = jnp.zeros_like(xown)
    xown[:, :CIN, :] = cot[...]
    xown[:, 80:84, :] = static[...]
    odd = (lax.axis_index("row") & 1) == 1
    pa[...] = xown[pl.ds(jnp.where(odd, 0, TR - HR), HR)]
    pb[...] = xown[pl.ds(jnp.where(odd, TR - HR, 0), HR)]


def own_rows(static, cot):
    return pl.pallas_call(
        rows_kernel,
        out_shape=[
            jax.ShapeDtypeStruct((TR, 128, 128), BF),
            jax.ShapeDtypeStruct((HR, 128, 128), BF),
            jax.ShapeDtypeStruct((HR, 128, 128), BF),
        ],
        in_specs=[VM] * 2,
        out_specs=[VM] * 3,
        cost_estimate=pl.CostEstimate(flops=0, bytes_accessed=2 * MB, transcendentals=0),
        compiler_params=pltpu.CompilerParams(vmem_limit_bytes=8 * MB),
        name="own_rows",
    )(static, cot)


def pack_kernel(ro, co, coarse, after, send, xs, prod, sem):
    ri = lax.axis_index("row")
    ci = col_place()
    first_row = ro[0] - 1 - LAT_DEV * ri
    off = co[0] - 1 - LON_DEV * ci
    start = jnp.clip(first_row, 0, LAT_DEV - 18)
    copy = pltpu.make_async_copy(coarse.at[pl.ds(start, 18)], xs, sem)
    copy.start()
    lj = iota((144, LON_DEV), 1)
    q = iota((144, LON_DEV), 0)
    tail = q - 80
    j_tail = jnp.where((tail & 7) < 6, 8 * (tail >> 3) + 8 + (tail & 1), -100000)
    j = jnp.where(q < 80, jnp.where(q < 66, q, -100000), j_tail)
    sel = one_hot(lj == off + j)
    prod[:, :, CIN:] = jnp.zeros((18, 144, 128 - CIN), F32)
    copy.wait()

    def rows(g, _):
        for k in range(6):
            i = 6 * g + k
            li = first_row + i
            ok = jnp.where((li >= 0) & (li < LAT_DEV), 1.0, 0.0)
            prod[i, :, :CIN] = dotf(sel, xs[jnp.clip(li - start, 0, 17)], NT) * ok
        return 0

    lax.fori_loop(0, 3, rows, 0)
    part = iota((144, 128), 1) >> 5
    low = iota((64, 128), 0) & 7

    def dest(r):
        ms = []
        for h in range(3):
            m = None
            for k in range(4):
                p = prod[2 * r + k]
                p = p if k == h else pltpu.roll(p, 32 * (k - h) % 128, 1)
                m = p if m is None else jnp.where(part == k, p, m)
            ms.append(m)
        tails = jnp.where(low < 2, ms[0][80:], jnp.where(low < 4, ms[1][80:], ms[2][80:]))
        for cc in range(8):
            d = (cc // 4) * 32 + r * 4 + cc % 4
            sl = slice(8 * cc, 8 * cc + 8)
            send[d] = jnp.concatenate([m[sl] for m in ms] + [tails[sl]], axis=0).astype(BF)

    def dests(g, _):
        for k in range(2):
            dest(2 * g + k)
        return 0

    lax.fori_loop(0, 4, dests, 0)


def pack(ro, co, coarse, after):
    return pl.pallas_call(
        pack_kernel,
        out_shape=jax.ShapeDtypeStruct((64, 32, 128), BF),
        in_specs=[SM, SM, pl.BlockSpec(memory_space=pltpu.HBM), pl.BlockSpec(memory_space=pl.ANY)],
        out_specs=VM,
        scratch_shapes=[
            pltpu.VMEM((18, CIN, LON_DEV), BF),
            pltpu.VMEM((18, 144, 128), F32),
            pltpu.SemaphoreType.DMA(()),
        ],
        cost_estimate=pl.CostEstimate(flops=0, bytes_accessed=8 * MB, transcendentals=0),
        compiler_params=pltpu.CompilerParams(vmem_limit_bytes=57 * MB),
        name="pack",
    )(ro, co, coarse, after)


def edge_kernel(xown, ra, rb, pc, pd, edge):
    odd = (lax.axis_index("row") & 1) == 1
    oddc = (col_place() & 1) == 1
    q = iota((16, 128), 0)
    sel = one_hot(iota((16, 128), 1) == jnp.where(q < 8, q, q + 112))

    def do(y0, x):
        n = x.shape[0]
        r = dotf(sel, x.reshape(n * 128, 128), NT)
        for k in range(n):
            edge[y0 + k] = r[:, k * 128 : (k + 1) * 128]

    do(HR, xown[...])
    a = ra[...]
    b = rb[...]
    do(0, jnp.where(odd, a, b))
    do(HR + TR, jnp.where(odd, b, a))
    left = edge[:, :8, :].reshape(ER * 8, 128)
    right = edge[:, 8:, :].reshape(ER * 8, 128)
    pc[...] = jnp.where(oddc, left, right).astype(BF)
    pd[...] = jnp.where(oddc, right, left).astype(BF)


def edges(xown, ra, rb):
    return pl.pallas_call(
        edge_kernel,
        out_shape=[
            jax.ShapeDtypeStruct((ER * 8, 128), BF),
            jax.ShapeDtypeStruct((ER * 8, 128), BF),
        ],
        in_specs=[VM] * 3,
        out_specs=[VM] * 2,
        scratch_shapes=[pltpu.VMEM((ER, 16, 128), F32)],
        cost_estimate=pl.CostEstimate(flops=0, bytes_accessed=4 * MB, transcendentals=0),
        compiler_params=pltpu.CompilerParams(vmem_limit_bytes=8 * MB),
        name="edges",
    )(xown, ra, rb)


def cells_kernel(xown, ra, rb, rc, rd, ct):
    odd = (lax.axis_index("row") & 1) == 1
    oddc = (col_place() & 1) == 1
    perm = one_hot(ext_col(iota((EC, 128), 0)) - HC == iota((EC, 128), 1))
    m = iota((2 * EC, 16), 0)
    q = iota((2 * EC, 16), 1)
    y2 = (m >= EC).astype(jnp.int32)
    e2 = ext_col(m - y2 * EC)
    same = y2 == (q >> 3)
    perm_l = one_hot(same & (e2 == (q & 7)))
    perm_r = one_hot(same & (e2 - (HC + TC) == (q & 7)))

    def do(y, x):
        rows = pl.ds(pl.multiple_of(y * 8, 16), 16)
        c = rc[rows, :]
        d = rd[rows, :]
        halo = dotf(perm_l, jnp.where(oddc, c, d)) + dotf(perm_r, jnp.where(oddc, d, c))
        for k in range(2):
            ct[y + k] = (dotf(perm, x[k], NT) + halo[k * EC : (k + 1) * EC]).astype(BF)

    def mid(i, _):
        for k in range(2):
            y = 4 * i + 2 * k
            do(y + HR, xown[pl.ds(y, 2)])
        return 0

    lax.fori_loop(0, TR // 4, mid, 0)
    for y in range(0, HR, 2):
        a = ra[y : y + 2]
        b = rb[y : y + 2]
        do(y, jnp.where(odd, a, b))
        do(y + HR + TR, jnp.where(odd, b, a))


def cells(xown, ra, rb, rc, rd):
    return pl.pallas_call(
        cells_kernel,
        out_shape=jax.ShapeDtypeStruct((ER, EC, 128), BF),
        in_specs=[VM] * 5,
        out_specs=VM,
        cost_estimate=pl.CostEstimate(flops=0, bytes_accessed=8 * MB, transcendentals=0),
        compiler_params=pltpu.CompilerParams(vmem_limit_bytes=8 * MB),
        name="cells",
    )(xown, ra, rb, rc, rd)


def fold_kernel(recv, out):
    out[...] = jnp.sum(recv[...].astype(F32), axis=0).astype(BF)


def fold(recv):
    return pl.pallas_call(
        fold_kernel,
        out_shape=jax.ShapeDtypeStruct((32, 128), BF),
        in_specs=[VM],
        out_specs=VM,
        compiler_params=pltpu.CompilerParams(vmem_limit_bytes=4 * MB),
        name="fold",
    )(recv)


def spread_kernel(mine, other, out):
    o = (mine[...] + other[...]).astype(BF)
    for d in range(64):
        out[d] = o


def spread(mine, other):
    return pl.pallas_call(
        spread_kernel,
        out_shape=jax.ShapeDtypeStruct((64, 32, 128), BF),
        in_specs=[VM] * 2,
        out_specs=VM,
        compiler_params=pltpu.CompilerParams(vmem_limit_bytes=4 * MB),
        name="spread",
    )(mine, other)


def main_kernel(
    win_a, win_b, ct, wbig, gains, kern_hbm, wl, deep_out, msg,
    vup, hid_a, hid_b, act_a, act_b, act_c, cv, hs_s, ds_s, gsum, kern, pair, sem,
):
    ri = lax.axis_index("row")
    ci = col_place()
    load = pltpu.make_async_copy(kern_hbm, kern, sem.at[0])
    load.start()

    win = win_a[...].astype(F32) + win_b[...].astype(F32)
    odd = (ri & 1) == 1
    win = jnp.where(odd, pltpu.roll(win, 96, 1), win)
    m = iota((EC, 96), 0)
    q = iota((EC, 96), 1)
    h = q >> 5
    q = q & 31
    j = jnp.where((q >> 3) == h, q & 7, jnp.where((q >> 1) == 12 + h, 8 + (q & 1), -10))
    coef = col_weight(ext_col(m), j).astype(BF)
    lane = iota((32, 128), 1)
    for k in range(3):
        parts = []
        for h in range(3):
            w = win if h == k else pltpu.roll(win, 32 * (h - k) % 128, 1)
            parts.append(jnp.where(((lane >> 5) == h) & (lane < CIN), w, 0.0))
        vup[k] = dotf(coef, jnp.concatenate(parts, axis=0).astype(BF))

    CK = 48
    col_ok = []
    for ck in range(3):
        gc = ci * TC + ext_col(iota((CK, 1), 0) + ck * CK) - HC
        col_ok.append(jnp.where((gc >= 0) & (gc < 8 * TC), 1.0, 0.0))

    def put(act, y, ck, v):
        act[y, 1 + 3 * ck : 4 + 3 * ck] = v.reshape(3, S, W)
        if ck == 2:
            act[y, 0] = pltpu.roll(v[32:48].astype(F32), 1, 0).astype(BF)
        if ck == 0:
            act[y, L + 1] = pltpu.roll(v[:16].astype(F32), S - 1, 0).astype(BF)

    def lane_mean(v):
        half = (v[:, :128] + v[:, 128:]).astype(F32)
        return jnp.sum(half, axis=-1, keepdims=True) * (1.0 / W)

    def over_lanes(v):
        half = jnp.broadcast_to(v, (v.shape[0], 128)).astype(BF)
        return jnp.concatenate([half, half], axis=1)

    def activate(b, y, ck, before, after, act):
        gr = ri * TR + y - HR
        ok = jnp.where((gr >= 0) & (gr < 16 * TR), 1.0, 0.0)
        gain = gains[pl.ds(jnp.minimum(b, BLOCKS - 1), 1), :].astype(BF)
        keep = jnp.clip(y - 3, 0, 21)
        sl = slice(ck * CK, (ck + 1) * CK)
        h = cv[y, sl]
        if before is not None:
            h = h + before[y, sl]
        after[y, sl] = h
        s = over_lanes(lax.rsqrt(lane_mean(h * h) + 1e-06) * (col_ok[ck] * ok))
        hs = h * s
        n = hs * gain
        half = BF(0.5)
        g = half * jnp.tanh(half * n) + half
        a = n * g
        put(act, y, ck, a)
        hs_s[b, keep, sl] = hs
        ds_s[b, keep, sl] = (g + a - a * g) * (gain * s)

    def lift(g):
        ups = []
        for k in range(4):
            n = 2 * (g * 4 + k) + 5
            a = n >> 5
            t = (n & 31).astype(F32) * (1.0 / 32.0)
            ups.append(((1.0 - t) * vup[a] + t * vup[a + 1]).astype(BF))
        up = jnp.concatenate(ups, axis=0)
        own = ct[pl.ds(g * 4, 4)].reshape(4 * EC, 128)
        r = dotf(jnp.concatenate([up, own], axis=1), wbig[...])
        r = r.astype(BF)
        cv[pl.ds(g * 4, 4)] = r[:, :W].reshape(4, EC, W)
        for k in range(4):
            for ck in range(3):
                put(act_c, g * 4 + k, ck, r[k * EC + ck * CK : k * EC + (ck + 1) * CK, W:])

    def start4(g):
        for k in range(4):
            for ck in range(3):
                activate(0, g * 4 + k, ck, None, hid_a, act_a)

    def pair_kernels(i):
        i = jnp.minimum(i, 3 * BLOCKS - 1)
        b = i // 3
        q = i - 3 * b
        for c in range(0, W, 64):
            sl = slice(c, c + 64)
            k0, k1, k2 = (kern[b, p, q, sl].astype(F32) for p in range(3))
            both = 0.5 * (k0 + k2)
            mid = 0.5 * k1
            pair[b, 0, q, sl] = (both + mid).astype(BF)
            pair[b, 1, q, sl] = (both - mid).astype(BF)

    def lift_on(g, _):
        start4(g - 1)
        lift(jnp.minimum(g, ER // 4 - 1))
        pair_kernels(2 * g - 2)
        pair_kernels(2 * g - 1)
        return 0

    lift(jnp.int32(0))
    load.wait()
    lax.fori_loop(1, ER // 4 + 1, lift_on, 0)

    def conv(b, act, y0, transpose, between=(), count=4):
        between = list(between)
        dims = NT if transpose else NN

        def rows(k):
            return jnp.concatenate([act[pl.ds(y0 - 1 + k + 2 * u, 1)] for u in range(count)], axis=0)

        d0, d1, d2, d3 = rows(0), rows(1), rows(2), rows(3)
        ms = []
        for k, t in enumerate((d0 - d2, d1 + d2, d2 - d1, d1 - d3)):
            acc = None
            for q in range(3):
                dx = 2 - q if transpose else q
                if k == 1 or k == 2:
                    kk = pair[b, k - 1, q]
                else:
                    kk = kern[b, 0 if (k == 3) == transpose else 2, q]
                r = dotf(t[:, dx : dx + L].reshape(count * EC, W), kk, dims)
                acc = r if acc is None else acc + r
                for job in between[:2]:
                    job()
                between = between[2:]
            ms.append(acc)
        e = (ms[0] + ms[1] + ms[2]).reshape(count, EC, W)
        o = (ms[1] - ms[2] - ms[3]).reshape(count, EC, W)
        for u in range(count):
            cv[y0 + 2 * u] = e[u].astype(BF)
            cv[y0 + 2 * u + 1] = o[u].astype(BF)

    def layer(b, lo, hi, act, transpose, after, short):
        back = 2 if short else 0

        def place(i):
            return jnp.minimum(lo + jnp.maximum(8 * i - back, 0), hi - 8)

        def rest(i):
            y0 = place(i)
            return [functools.partial(after, y0 + k, ck) for k in range(8) for ck in range(3)]

        def unit(i, _):
            conv(b, act, place(i), transpose, rest(i - 1))
            return 0

        n = (hi - lo + back + 7) >> 3
        conv(b, act, lo, transpose, (), 3 if short else 4)
        lax.fori_loop(1, n, unit, 0)
        for job in rest(n - 1):
            job()

    def forward(i, _):
        for b, src, dst in ((2 * i, (hid_a, act_a), (hid_b, act_b)), (2 * i + 1, (hid_b, act_b), (hid_a, act_a))):
            deep = b == 3
            lo = jnp.where(deep, HR, b + 1)
            hi = jnp.where(deep, HR + TR, ER - 1 - b)

            def after(y, ck, b=b, src=src, dst=dst):
                activate(b + 1, y, ck, src[0], *dst)

            layer(b, lo, hi, src[1], False, after, dst[0] is hid_b)
        return 0

    lax.fori_loop(0, 2, forward, 0)

    save = pltpu.make_async_copy(hid_a.at[pl.ds(HR, TR)], deep_out, sem.at[1])
    save.start()

    def grad(b, y, ck, before, act):
        sl = slice(ck * CK, (ck + 1) * CK)
        u = cv[y, sl] * ds_s[b, y - 3, sl]
        hs = hs_s[b, y - 3, sl]
        old = before[y, 1 + 3 * ck : 4 + 3 * ck].reshape(CK, W)
        put(act, y, ck, old + (u - hs * over_lanes(lane_mean(u * hs))))

    def backward(i, _):
        for b, src, dst in ((3 - 2 * i, act_c, act_a), (2 - 2 * i, act_a, act_c)):

            def after(y, ck, b=b, src=src, dst=dst):
                grad(b, y, ck, src, dst)

            layer(b, HR - b, HR + TR + b, src, True, after, dst is act_a)
        return 0

    lax.fori_loop(0, 2, backward, 0)

    e = ext_col(iota((32, EC), 1))
    qq = iota((32, EC), 0)
    j = jnp.where(qq < 10, qq, jnp.where(qq < 20, qq - 10, jnp.where(qq < 30, qq - 20, -10)))
    own = (e >= HC) & (e < HC + TC)
    cols_t = jnp.where(own, col_weight(e, j), 0.0).astype(BF)
    gsum[...] = jnp.zeros_like(gsum)

    def gather(g, _):
        for k in range(4):
            y = 4 * g + k + HR
            t = dotf(cols_t, act_c[y, 1 : 1 + L].reshape(EC, W))
            n = 2 * y + 5
            a = n >> 5
            w = (n & 31).astype(F32) * (1.0 / 32.0)
            gsum[a] = gsum[a] + (1.0 - w) * t
            gsum[a + 1] = gsum[a + 1] + w * t
        return 0

    lax.fori_loop(0, TR // 4, gather, 0)
    g = jnp.concatenate([gsum[0], gsum[1], gsum[2]], axis=1)
    g_hi = g.astype(BF)
    g_lo = (g - g_hi.astype(F32)).astype(BF)
    o = dotf(g_hi, wl[...]) + dotf(g_lo, wl[...])
    row = iota((32, 128), 0)
    o = jnp.where(row < 10, o[:, :128], jnp.where(row < 20, o[:, 128:256], o[:, 256:]))
    msg[...] = jnp.where(odd, pltpu.roll(o, 32, 1), o)
    save.wait()


def main(win_a, win_b, ct, wbig, gains, kern, wl):
    return pl.pallas_call(
        main_kernel,
        out_shape=[
            jax.ShapeDtypeStruct((TR, EC, W), BF),
            jax.ShapeDtypeStruct((32, 128), F32),
        ],
        in_specs=[VM] * 5 + [pl.BlockSpec(memory_space=pl.ANY), VM],
        out_specs=[pl.BlockSpec(memory_space=pltpu.HBM), VM],
        scratch_shapes=[
            pltpu.VMEM((3, EC, 128), F32),
            pltpu.VMEM((ER, EC, W), BF),
            pltpu.VMEM((ER, EC, W), BF),
            pltpu.VMEM((ER, L + 2, S, W), BF),
            pltpu.VMEM((ER, L + 2, S, W), BF),
            pltpu.VMEM((ER, L + 2, S, W), BF),
            pltpu.VMEM((ER, EC, W), BF),
            pltpu.VMEM((BLOCKS + 1, ER - 6, EC, W), BF),
            pltpu.VMEM((BLOCKS + 1, ER - 6, EC, W), BF),
            pltpu.VMEM((3, 32, W), F32),
            pltpu.VMEM((BLOCKS, 3, 3, W, W), BF),
            pltpu.VMEM((BLOCKS, 2, 3, W, W), BF),
            pltpu.SemaphoreType.DMA((2,)),
        ],
        compiler_params=pltpu.CompilerParams(vmem_limit_bytes=50 * MB),
        name="main",
    )(win_a, win_b, ct, wbig, gains, kern, wl)


def head_kernel(hid, wht, after, fine, mixed):
    perm = one_hot(ext_col(iota((EC, TC), 0)) - HC == iota((EC, TC), 1))
    for y in range(TR):
        mixed[y] = dotf(wht[...], hid[y], NT).astype(BF)
    out = dotf(mixed[...].reshape(TR * 80, EC), perm).astype(BF).reshape(TR, 80, TC)
    fine[...] = out[:, :CIN]


def head(hid, wht, after):
    return pl.pallas_call(
        head_kernel,
        out_shape=jax.ShapeDtypeStruct((TR, CIN, TC), BF),
        in_specs=[VM, VM, pl.BlockSpec(memory_space=pl.ANY)],
        out_specs=VM,
        scratch_shapes=[pltpu.VMEM((TR, 80, EC), BF)],
        cost_estimate=pl.CostEstimate(flops=0, bytes_accessed=6 * MB, transcendentals=0),
        compiler_params=pltpu.CompilerParams(vmem_limit_bytes=8 * MB),
        name="head",
    )(hid, wht, after)


def blank_kernel(after, out):
    out[...] = jnp.zeros_like(out)


def blank(after):
    return pl.pallas_call(
        blank_kernel,
        out_shape=jax.ShapeDtypeStruct((LAT_DEV, CIN, LON_DEV), F32),
        grid=(5,),
        in_specs=[pl.BlockSpec(memory_space=pl.ANY)],
        out_specs=pl.BlockSpec((9, CIN, LON_DEV), lambda i: (i, 0, 0)),
        cost_estimate=pl.CostEstimate(flops=0, bytes_accessed=4 * MB, transcendentals=0),
        compiler_params=pltpu.CompilerParams(vmem_limit_bytes=8 * MB),
        name="blank",
    )(after)


def place_kernel(ro, co, recv, zero, out, acc, sem):
    first_row = ro[0] - 1 - LAT_DEV * lax.axis_index("row")
    off = co[0] - 1 - LON_DEV * col_place()
    q = iota((256, 768), 0)
    lane = iota((256, 768), 1)
    lj = lane & 255
    j = (q & 31) - 10 * (lane >> 8)
    sel = one_hot((j >= 0) & (j < 10) & (lj == off + 8 * (q >> 5) + j) & (lj < LON_DEV))
    acc[...] = jnp.zeros_like(acc)

    def rows(g, _):
        for u in range(4):
            r = 4 * g + u
            o = dotf(recv[:, r].reshape(256, 128), sel, TN)
            for k in range(4):
                for h in range(3):
                    n = min(32, CIN - 32 * h)
                    sl = slice(32 * h, 32 * h + n)
                    part = o[32 * k : 32 * k + n, 256 * h : 256 * h + LON_DEV]
                    acc[2 * r + k, sl] = acc[2 * r + k, sl] + part
        return 0

    lax.fori_loop(0, 2, rows, 0)
    lo = jnp.clip(-first_row, 0, 18)
    hi = jnp.clip(LAT_DEV - first_row, lo, 18)

    def copy(i):
        li = jnp.clip(first_row + i, 0, LAT_DEV - 1)
        return pltpu.make_async_copy(acc.at[i], out.at[li], sem)

    def start(i, _):
        copy(i).start()
        return 0

    def wait(i, _):
        copy(i).wait()
        return 0

    lax.fori_loop(lo, hi, start, 0)
    lax.fori_loop(lo, hi, wait, 0)


def place(ro, co, recv, zero):
    hbm = pl.BlockSpec(memory_space=pltpu.HBM)
    return pl.pallas_call(
        place_kernel,
        out_shape=jax.ShapeDtypeStruct((LAT_DEV, CIN, LON_DEV), F32),
        in_specs=[SM, SM, VM, hbm],
        out_specs=hbm,
        input_output_aliases={3: 0},
        scratch_shapes=[pltpu.VMEM((18, CIN, LON_DEV), F32), pltpu.SemaphoreType.DMA(())],
        compiler_params=pltpu.CompilerParams(vmem_limit_bytes=16 * MB),
        name="place",
    )(ro, co, recv, zero)


def shards(coarse, ro, co, static, w_lift, w_static, gains, kern, w_head, cot):
    xown, pa, pb = own_rows(static, cot)
    near = [(i, i ^ 1) for i in range(16)]
    far = [(i, j) for i in range(16) for j in [i + 1 if i & 1 else i - 1] if 0 <= j < 16]
    ra = lax.ppermute(pa, "row", near)
    rb = lax.ppermute(pb, "row", far)
    send = pack(ro, co, coarse, pa)
    pc, pd = edges(xown, ra, rb)
    near = [(i, i ^ 1) for i in range(8)]
    far = [(i, j) for i in range(8) for j in [i + 1 if i & 1 else i - 1] if 0 <= j < 8]
    send, pc, pd = lax.optimization_barrier((send, pc, pd))
    rc = lax.ppermute(pc, ("sec", "col"), near)
    rd = lax.ppermute(pd, ("sec", "col"), far)
    groups = [
        [sec * 64 + row * 4 + col for sec in range(2) for row in range(core, 16, 2) for col in range(4)]
        for core in range(2)
    ]

    def swap(x):
        return lax.all_to_all(x, ("sec", "row", "col"), 0, 0, axis_index_groups=groups, tiled=True)

    mates = [(i, i ^ 1) for i in range(16)]
    win_a = fold(swap(send))
    win_b = lax.ppermute(win_a, "row", mates)
    ct = cells(xown, ra, rb, rc, rd)

    wht = w_head.T
    zero = jnp.zeros
    wbig = jnp.concatenate(
        [
            jnp.concatenate([w_lift, zero((50, W), BF), zero((80, W), BF), w_static, zero((44, W), BF)], 0),
            jnp.concatenate([zero((128, W), BF), wht, zero((50, W), BF)], 0),
        ],
        1,
    )
    wht80 = jnp.concatenate([wht, zero((2, W), BF)], 0)
    wl = jnp.concatenate([w_lift, zero((18, W), BF)], 0).reshape(3, 32, W).transpose(2, 0, 1)
    wl = jnp.concatenate(
        [jnp.pad(wl, ((0, 0), (0, 0), (32 * k, 96 - 32 * k))).reshape(W, 384) for k in range(3)], 0
    )
    deep, own = main(win_a, win_b, ct, wbig, gains, kern, wl)
    msg = spread(own, lax.ppermute(own, "row", mates))
    back = swap(msg)
    return head(deep, wht80, msg), place(ro, co, back.reshape(2, 8, 4, 32, 128), blank(msg))


def solution(mesh):
    tile = P("row", None, ("sec", "col"))
    in_specs = (tile, P(), P(), tile, P(), P(), P(), P(), P(), tile)
    return jax.shard_map(shards, mesh=mesh, in_specs=in_specs, out_specs=(tile, tile), check_vma=False)
```
